128 devices in a mesh: dp: 16 (over y_hi, z, core), tensor: 8 (over x, y_lo).
Axes of the slice: x: 4, y: 4 (y_hi: 2, y_lo: 2; y = y_hi * 2 + y_lo), z: 4, core: 2. Of those that a mesh axis runs over, the one named last changes fastest.
Arguments:
- x_rows: bfloat16 [3072, 16384], P(('dp', 'tensor')), may hold values from -6 to 6
- w_key: bfloat16 [16384, 512], P('dp', 'tensor'), may hold values from -0.046875 to 0.046875
- w_value: bfloat16 [16384, 512], P('dp', 'tensor'), may hold values from -0.046875 to 0.046875
- w_query: bfloat16 [16384, 8192], P('dp', 'tensor'), may hold values from -0.046875 to 0.046875
- queries: bfloat16 [3072, 8192], P('dp', 'tensor'), may hold values from -4 to 4
- grad_out: bfloat16 [3072, 8192], P('dp', 'tensor'), may hold values from -6 to 6
- segment_ids: int32 [16, 192], P('dp'), may hold values from 0 to 7, never falling along the last dimension, each value on 1 to 96 neighbouring positions
Outputs:
- grad_queries: bfloat16 [3072, 8192], P('dp', 'tensor')
- grad_rows: bfloat16 [3072, 16384], P(('dp', 'tensor'))
- grad_key_weight: float32 [16384, 512], P('dp', 'tensor')
- grad_value_weight: float32 [16384, 512], P('dp', 'tensor')
- grad_query_weight: float32 [16384, 8192], P('dp', 'tensor')
The draws below stay inside these ranges and needn't reach their ends.
Inputs may be any that keep to these rules, and one draw needn't show every extreme that they name: `segment_ids`: in each rollout batch the document numbers never fall, each of the 8 documents holds 1 to 96 tokens, and one holds exactly 96.
All inputs are finite; a program needn't handle non-finite values.
Results may differ from the reference program's by a relative error of at most 0.038.
Values may be sent and summed in bfloat16 or wider, within the bound.
A program may use at most 128 MiB of HBM per device.

```python
import math
import jax
import jax.numpy as jnp
import numpy as np
from jax import lax

D = 16384
HD = 128
HEADS_DEV = 8
TOK = 192
DOCS = 8
HQ = 64
KV = 4
N_DP = 16
N_TENSOR = 8


def block_levels(rng, shape, shards, low, top_value):
    loudness = 1.0
    for dim, blocks in shards:
        draws = jax.random.uniform(jax.random.fold_in(jax.random.fold_in(rng, 6), dim), (blocks,), jnp.float32, low / len(shards), top_value / len(shards))
        loudness = loudness * jnp.repeat(jnp.exp(draws), shape[dim] // blocks).reshape((-1,) + (1,) * (len(shape) - 1 - dim))
    return loudness


def profile(count, total, most, skew):
    portions = [(1 << 20) // math.isqrt(standing ** skew) + 1 for standing in range(2, count + 1)]
    surplus, given = total - most - (count - 1), [1] * (count - 1)
    while surplus > 0:
        movable = [i for i in range(count - 1) if given[i] < most]
        whole, budget = sum([portions[i] for i in movable]), surplus
        for i in movable:
            extra = min(most - given[i], max(1, budget * portions[i] // whole), surplus)
            given[i] = given[i] + extra
            surplus = surplus - extra
    return np.array([most] + given)


def uneven_parts(key, number_of, total, bound, skew):
    if number_of == 2:
        one = jax.random.randint(key, (), max(1, total - bound), min(bound, total - 1) + 1)
        return jnp.stack([one, total - one])
    tallies = jnp.asarray(profile(number_of, total, bound, skew), jnp.int32)
    couples = (number_of - 1) // 2
    giver, receiver = tallies[1:1 + 2 * couples:2], tallies[2:2 + 2 * couples:2]
    margin = jnp.minimum(giver - 1, bound - receiver)
    passed = jax.random.randint(jax.random.fold_in(key, 1), (couples,), 0, 1 << 20) % (margin + 1)
    tallies = tallies.at[1:1 + 2 * couples:2].set(giver - passed).at[2:2 + 2 * couples:2].set(receiver + passed)
    return tallies[jax.random.permutation(jax.random.fold_in(key, 2), number_of)]


def bell_draw(key, extent, spread, most, split=(), held_as=jnp.bfloat16):
    array = spread * jax.random.normal(key, extent, jnp.float32)
    if split:
        array = array * block_levels(key, extent, split, -0.22, 0.18)
    return jnp.clip(array, -most, most).astype(held_as)


def setup_inputs(seed: int = 0) -> dict:
    key_list = jax.random.split(jax.random.key(seed), 8)
    x_rows = bell_draw(key_list[0], (N_DP * TOK, D), 1.0, 6.0, ((0, 128),))
    w_key = bell_draw(key_list[1], (D, KV * HD), D ** -0.5, 0.046875, ((0, 16), (1, 8)))
    w_value = bell_draw(key_list[2], (D, KV * HD), D ** -0.5, 0.046875, ((0, 16), (1, 8)))
    w_query = bell_draw(key_list[3], (D, HQ * HD), D ** -0.5, 0.046875, ((0, 16), (1, 8)))
    queries = bell_draw(key_list[4], (N_DP * TOK, HQ * HD), 1.0, 4.0, ((0, 16), (1, 8)))
    grad_out = bell_draw(key_list[5], (N_DP * TOK, HQ * HD), 1.0, 6.0, ((0, 16), (1, 8)))
    segment_ids = jax.vmap(lambda own: jnp.searchsorted(jnp.cumsum(uneven_parts(own, DOCS, TOK, TOK // 2, 2)), jnp.arange(TOK), side="right"))(jax.random.split(key_list[6], N_DP)).reshape((N_DP, TOK)).astype(jnp.int32)
    return dict(x_rows=x_rows, w_key=w_key, w_value=w_value, w_query=w_query, queries=queries, grad_out=grad_out, segment_ids=segment_ids)


theta_base = 500000.0


def rotary_tables(segment_row):
    count = segment_row.shape[0]
    places = jnp.arange(count, dtype=jnp.int32)
    earlier = jnp.concatenate([segment_row[:1] - 1, segment_row[:-1]])
    starts = lax.cummax(jnp.where(segment_row != earlier, places, 0), axis=0)
    position = (places - starts).astype(jnp.float32)
    half = HD // 2
    freqs = theta_base ** (-(2.0 * jnp.arange(half, dtype=jnp.float32)) / HD)
    angles = position[:, None] * freqs[None, :]
    allowed = (segment_row[:, None] == segment_row[None, :]) & (places[None, :] <= places[:, None])
    return jnp.cos(angles), jnp.sin(angles), allowed


def block_grads(x_block, query_block, dout_block, segment_row, w_key, w_value):
    half = HD // 2
    group = HQ // KV
    scale = 1.0 / (HD ** 0.5)
    cosine, sine, allowed = rotary_tables(segment_row)
    cos3 = cosine[:, None, :]
    sin3 = sine[:, None, :]
    key_lin = jnp.dot(x_block, w_key, preferred_element_type=jnp.float32).astype(jnp.bfloat16)
    values = jnp.dot(x_block, w_value, preferred_element_type=jnp.float32).astype(jnp.bfloat16)
    key_heads = key_lin.reshape(TOK, KV, HD).astype(jnp.float32)
    first = key_heads[..., :half]
    second = key_heads[..., half:]
    keys = jnp.concatenate([first * cos3 - second * sin3, second * cos3 + first * sin3], axis=-1).astype(jnp.bfloat16)
    keys_f = keys.astype(jnp.float32)
    values_f = values.reshape(TOK, KV, HD).astype(jnp.float32)
    query_f = query_block.reshape(TOK, KV, group, HD).astype(jnp.float32)
    dout_f = dout_block.reshape(TOK, KV, group, HD).astype(jnp.float32)
    scores = jnp.einsum("tgjd,sgd->gjts", query_f, keys_f) * scale
    weights = jnp.where(allowed, jnp.exp(scores), 0.0)
    probs = weights / jnp.sum(weights, axis=-1, keepdims=True)
    dprob = jnp.einsum("tgjd,sgd->gjts", dout_f, values_f)
    delta = jnp.sum(probs * dprob, axis=-1, keepdims=True)
    dscore = (probs * (dprob - delta)).astype(jnp.bfloat16).astype(jnp.float32)
    probs_low = probs.astype(jnp.bfloat16).astype(jnp.float32)
    grad_q = (jnp.einsum("gjts,sgd->tgjd", dscore, keys_f) * scale).astype(jnp.bfloat16)
    grad_key_rot = jnp.einsum("gjts,tgjd->sgd", dscore, query_f) * scale
    grad_value_f = jnp.einsum("gjts,tgjd->sgd", probs_low, dout_f)
    upper = grad_key_rot[..., :half]
    lower = grad_key_rot[..., half:]
    grad_key_lin = jnp.concatenate([upper * cos3 + lower * sin3, lower * cos3 - upper * sin3], axis=-1)
    grad_key_lin = grad_key_lin.reshape(TOK, KV * HD).astype(jnp.bfloat16)
    grad_value = grad_value_f.reshape(TOK, KV * HD).astype(jnp.bfloat16)
    return grad_q.reshape(TOK, HQ * HD), grad_key_lin, grad_value


def row_grads(grad_q, grad_key_lin, grad_value, w_query, w_key, w_value):
    half = HD // 2
    query_width = HEADS_DEV * HD
    query_parts = grad_q.reshape(TOK, N_TENSOR, query_width)
    wquery_parts = w_query.reshape(D, N_TENSOR, query_width)
    key_parts = grad_key_lin.reshape(TOK, N_TENSOR, half)
    value_parts = grad_value.reshape(TOK, N_TENSOR, half)
    wkey_parts = w_key.reshape(D, N_TENSOR, half)
    wvalue_parts = w_value.reshape(D, N_TENSOR, half)

    def add_group(total, index):
        term = jnp.dot(query_parts[:, index], wquery_parts[:, index].T, preferred_element_type=jnp.float32)
        term = term + jnp.dot(key_parts[:, index], wkey_parts[:, index].T, preferred_element_type=jnp.float32)
        term = term + jnp.dot(value_parts[:, index], wvalue_parts[:, index].T, preferred_element_type=jnp.float32)
        return total + term.astype(jnp.bfloat16).astype(jnp.float32), None

    total, unused = lax.scan(add_group, jnp.zeros((TOK, D), jnp.float32), jnp.arange(N_TENSOR, dtype=jnp.int32))
    return total.astype(jnp.bfloat16)


def reference(x_rows, w_key, w_value, w_query, queries, grad_out, segment_ids):
    x_blocks = x_rows.reshape(N_DP, TOK, D)
    query_blocks = queries.reshape(N_DP, TOK, HQ * HD)
    dout_blocks = grad_out.reshape(N_DP, TOK, HQ * HD)

    def step(carry, items):
        x_block = items[0]
        grad_q, grad_key_lin, grad_value = block_grads(x_block, items[1], items[2], items[3], w_key, w_value)
        grad_x = row_grads(grad_q, grad_key_lin, grad_value, w_query, w_key, w_value)
        key_weight = carry[0] + jnp.dot(x_block.T, grad_key_lin, preferred_element_type=jnp.float32)
        value_weight = carry[1] + jnp.dot(x_block.T, grad_value, preferred_element_type=jnp.float32)
        query_weight = carry[2] + jnp.dot(x_block.T, grad_q, preferred_element_type=jnp.float32)
        return (key_weight, value_weight, query_weight), (grad_q, grad_x)

    start = (jnp.zeros((D, KV * HD), jnp.float32), jnp.zeros((D, KV * HD), jnp.float32), jnp.zeros((D, HQ * HD), jnp.float32))
    sums, stacked = lax.scan(step, start, (x_blocks, query_blocks, dout_blocks, segment_ids))
    grad_queries = stacked[0].reshape(N_DP * TOK, HQ * HD)
    grad_rows = stacked[1].reshape(N_DP * TOK, D)
    return grad_queries, grad_rows, sums[0], sums[1], sums[2]
```

```python
import jax
import jax.numpy as jnp
from jax import lax
from jax.sharding import PartitionSpec as P

theta_base = 500000.0


def partner(block, axis, distance):
    count = lax.axis_size(axis)
    route = []
    for low in range(count):
        high = low | 1 << distance
        if high != low and high < count:
            route += [(low, high), (high, low)]
    return lax.ppermute(block, axis, route)


def rotary_tables(segment_row, head_dim):
    count = segment_row.shape[0]
    places = jnp.arange(count, dtype=jnp.int32)
    earlier = jnp.concatenate([segment_row[:1] - 1, segment_row[:-1]])
    starts = lax.cummax(jnp.where(segment_row != earlier, places, 0), axis=0)
    position = (places - starts).astype(jnp.float32)
    half = head_dim // 2
    freqs = theta_base ** (-(2.0 * jnp.arange(half, dtype=jnp.float32)) / head_dim)
    angles = position[:, None] * freqs[None, :]
    allowed = (segment_row[:, None] == segment_row[None, :]) & (places[None, :] <= places[:, None])
    return (jnp.cos(angles), jnp.sin(angles), allowed)


def shards(x_rows, w_key, w_value, w_query, queries, grad_out, segment_ids):
    half = w_key.shape[1]
    head_dim = 2 * half
    tokens = queries.shape[0]
    heads = queries.shape[1] // head_dim
    scale = 1.0 / head_dim**0.5
    lower_half = lax.axis_index("tensor") % 2 == 0
    cosine, sine, allowed = rotary_tables(segment_ids[0], head_dim)
    own_rows = x_rows.shape[0]
    batches = lax.axis_size("dp")
    groups = lax.axis_size("tensor")
    own_tokens = lax.all_to_all(x_rows, "dp", split_axis=1, concat_axis=0, tiled=True)
    features = own_tokens.shape[1]
    columns = lax.all_gather(own_tokens, "tensor", axis=0, tiled=False)
    columns = columns.reshape(groups, batches, own_rows, features).transpose(1, 0, 2, 3)
    columns = columns.reshape(batches * tokens, features)
    joined = jnp.concatenate([w_key, w_value], axis=1)
    own_lin = lax.psum_scatter(
        jnp.dot(columns, joined, preferred_element_type=jnp.float32).astype(jnp.bfloat16),
        "dp",
        scatter_dimension=0,
        tiled=True,
    )
    partner_lin = partner(own_lin, "tensor", 0)
    first = jnp.where(lower_half, own_lin, partner_lin)
    second = jnp.where(lower_half, partner_lin, own_lin)
    key_first = first[:, :half]
    key_second = second[:, :half]
    values = jnp.concatenate([first[:, half:], second[:, half:]], axis=1)
    first_f = key_first.astype(jnp.float32)
    second_f = key_second.astype(jnp.float32)
    keys = jnp.concatenate(
        [first_f * cosine - second_f * sine, second_f * cosine + first_f * sine], axis=1
    ).astype(jnp.bfloat16)
    query_heads = queries.reshape(tokens, heads, head_dim)
    dout_heads = grad_out.reshape(tokens, heads, head_dim)
    scores = (
        jnp.einsum("thd,sd->hts", query_heads, keys, preferred_element_type=jnp.float32) * scale
    )
    weights = jnp.where(allowed[None], jnp.exp(scores), 0.0)
    probs = weights / jnp.sum(weights, axis=-1, keepdims=True)
    dprob = jnp.einsum("thd,sd->hts", dout_heads, values, preferred_element_type=jnp.float32)
    delta = jnp.sum(probs * dprob, axis=-1, keepdims=True)
    dscore = (probs * (dprob - delta)).astype(jnp.bfloat16)
    probs_low = probs.astype(jnp.bfloat16)
    grad_q = jnp.einsum("hts,sd->thd", dscore, keys, preferred_element_type=jnp.float32) * scale
    grad_queries = grad_q.astype(jnp.bfloat16).reshape(tokens, heads * head_dim)
    key_part = (
        jnp.einsum("hts,thd->sd", dscore, query_heads, preferred_element_type=jnp.float32) * scale
    )
    value_part = jnp.einsum(
        "hts,thd->sd", probs_low, dout_heads, preferred_element_type=jnp.float32
    )
    other_keyg, other_valueg = (
        partner(key_part.astype(jnp.bfloat16), "tensor", 0).astype(key_part.dtype),
        partner(value_part.astype(jnp.bfloat16), "tensor", 0).astype(value_part.dtype),
    )
    key_rot = key_part + other_keyg
    value_sum = value_part + other_valueg
    upper = key_rot[:, :half]
    lower = key_rot[:, half:]
    grad_key_lin = jnp.concatenate(
        [upper * cosine + lower * sine, lower * cosine - upper * sine], axis=1
    ).astype(jnp.bfloat16)
    grad_value = value_sum.astype(jnp.bfloat16)
    own_key = jnp.where(lower_half, grad_key_lin[:, :half], grad_key_lin[:, half:])
    own_value = jnp.where(lower_half, grad_value[:, :half], grad_value[:, half:])
    own_grad = jnp.concatenate([own_key, own_value], axis=1)
    all_query, all_own = (
        lax.all_gather(grad_queries, "dp", axis=0, tiled=True),
        lax.all_gather(own_grad, "dp", axis=0, tiled=True),
    )
    contract_rows = (((0,), (0,)), ((), ()))
    contract_cols = (((1,), (1,)), ((), ()))
    pair_weight = lax.dot_general(
        columns, all_own, contract_rows, preferred_element_type=jnp.float32
    )
    query_weight = lax.dot_general(
        columns, all_query, contract_rows, preferred_element_type=jnp.float32
    )
    term = lax.dot_general(all_query, w_query, contract_cols, preferred_element_type=jnp.float32)
    term = term + lax.dot_general(
        all_own, joined, contract_cols, preferred_element_type=jnp.float32
    )
    by_owner = term.astype(jnp.bfloat16).reshape(batches, groups, own_rows, features)
    by_owner = by_owner.transpose(1, 0, 2, 3).reshape(groups * batches * own_rows, features)
    reduced = lax.psum_scatter(by_owner, "tensor", scatter_dimension=0, tiled=True)
    grad_rows = lax.all_to_all(reduced, "dp", split_axis=0, concat_axis=1, tiled=True)
    return (grad_queries, grad_rows, pair_weight[:, :half], pair_weight[:, half:], query_weight)


def solution(mesh):
    placed = (
        P(("dp", "tensor"), None),
        P("dp", "tensor"),
        P("dp", "tensor"),
        P("dp", "tensor"),
        P("dp", "tensor"),
        P("dp", "tensor"),
        P("dp", None),
    )
    return jax.shard_map(
        shards,
        mesh=mesh,
        in_specs=placed,
        out_specs=(
            P("dp", "tensor"),
            P(("dp", "tensor"), None),
            P("dp", "tensor"),
            P("dp", "tensor"),
            P("dp", "tensor"),
        ),
        check_vma=False,
    )
```

```python
import functools

import jax
import jax.numpy as jnp
import numpy as np
from jax import lax
from jax.experimental import pallas as pl
from jax.experimental.pallas import tpu as pltpu
from jax.sharding import PartitionSpec as P

theta_base = 500000.0
MESH = pl.DeviceIdType.MESH
F32 = jnp.float32
BF16 = jnp.bfloat16

N_DP = 16
N_T = 8
ROWS = 24
TOK = 192
FEAT = 1024
COLS = 1024
HD = 128
HALF = 64
WIDE = COLS + HD
SLOTS = (0, 2, 6, 8, 10, 14, 4, 12)
ORDERS = ((1, 2, 6), (2, 6, 1), (6, 1, 2))


def xor_ring(place, mask):
    if mask == 0:
        return place
    if mask == 1:
        return place + 1 - 2 * lax.rem(place, 2)
    if mask == 2:
        return lax.rem(place + 2, 4)
    return 3 - place


def xor_dp(d, mask):
    y_hi, z, core = d // 8, lax.rem(d // 2, 4), lax.rem(d, 2)
    y_hi = 1 - y_hi if mask & 8 else y_hi
    core = 1 - core if mask & 1 else core
    return y_hi * 8 + xor_ring(z, (mask // 2) % 4) * 2 + core


def xor_t(t, mask):
    x, y_lo = t // 2, lax.rem(t, 2)
    y_lo = 1 - y_lo if mask & 1 else y_lo
    return xor_ring(x, mask // 2) * 2 + y_lo


def rows_at(start, size, unit):
    return pl.ds(pl.multiple_of(start, unit), size)


def remote(src, dst, send, recv, d, t):
    return pltpu.make_async_remote_copy(
        src_ref=src, dst_ref=dst, send_sem=send, recv_sem=recv, device_id=(d, t), device_id_type=MESH
    )


def fold(block):
    return jnp.concatenate([block[:, : FEAT // 2], block[:, FEAT // 2 :]], axis=0)


def unfold(block):
    return jnp.concatenate([block[:ROWS], block[ROWS:]], axis=1)


def dot_nt(a, b):
    return lax.dot_general(a, b, (((1,), (1,)), ((), ())), preferred_element_type=F32)


def dot_nn(a, b):
    return lax.dot_general(a, b, (((1,), (0,)), ((), ())), preferred_element_type=F32)


def dot_tn(a, b):
    return lax.dot_general(a, b, (((0,), (0,)), ((), ())), preferred_element_type=F32)


class Gather:
    def __init__(self, buf, slot_rows, chunks, send, recv, d, t):
        self.buf, self.slot_rows, self.chunks = buf, slot_rows, chunks
        self.send, self.recv, self.d, self.t = send, recv, d, t

    def copies(self, stage, arriving):
        out = []
        for c, (offset, size) in enumerate(self.chunks):
            first, second, third = ORDERS[c]
            held = ([0], [0, first], [0, first, second, first ^ second])[stage]
            link = ORDERS[c][stage]
            for j in held:
                slot = xor_t(self.t, j ^ link if arriving else j)
                part = self.buf.at[rows_at(slot * self.slot_rows + offset, size, 16)]
                n = (j ^ link) - 1
                out.append(
                    remote(part, part, self.send.at[c, n], self.recv.at[c, n], self.d, xor_t(self.t, link))
                )
        return out

    def start(self, stage):
        for copy in self.copies(stage, False):
            copy.start()

    def wait(self, stage):
        for copy in self.copies(stage, True):
            copy.wait_recv()

    def finish(self):
        for stage in range(3):
            for copy in self.copies(stage, False):
                copy.wait_send()


def front(
    x_ref, wk_ref, wv_ref, q_ref, do_ref, seg_ref, freq_ref,
    gq_ref, own_ref, xg,
    xsend, xa, wg, kvf, kvsend, kvrecv, heads_out, heads_in, part_out, part_in,
    cos_ref, sin_ref, mask_ref, keyp, valuep, key_ref, value_ref,
    x_s, x_r, w_s, w_r, g_s, g_r, kv_s, kv_r, h_s, h_r, p_s, p_r,
):
    d = lax.axis_index("dp")
    t = lax.axis_index("tensor")
    barrier = pltpu.get_barrier_semaphore()

    def greet_dp(k, carry):
        pl.semaphore_signal(barrier, inc=1, device_id=(lax.rem(d + k, N_DP), t), device_id_type=MESH)
        return carry

    def greet_t(k, carry):
        pl.semaphore_signal(barrier, inc=1, device_id=(d, lax.rem(t + k, N_T)), device_id_type=MESH)
        return carry

    lax.fori_loop(1, N_DP, greet_dp, 0)
    lax.fori_loop(1, N_T, greet_t, 0)
    wg[rows_at(t * HD, HALF, HALF)] = wk_ref[...]
    wg[rows_at(t * HD + HALF, HALF, HALF)] = wv_ref[...]
    pl.semaphore_wait(barrier, N_DP + N_T - 2)

    weights = Gather(wg, HD, ((0, 48), (48, 48), (96, 32)), w_s, w_r, d, t)
    weights.start(0)

    def x_copy(k, to):
        return remote(xsend.at[to], xa.at[d], x_s.at[k], x_r.at[k], to, t)

    def pack_x(k, carry):
        to = lax.rem(d + k, N_DP)
        block = x_ref[:, rows_at(to * FEAT, FEAT, FEAT)].astype(F32)
        xsend[to] = fold(block).astype(BF16)
        x_copy(k, to).start()
        return carry

    lax.fori_loop(1, N_DP, pack_x, 0)
    xa[d] = fold(x_ref[:, rows_at(d * FEAT, FEAT, FEAT)].astype(F32)).astype(BF16)
    weights.wait(0)
    weights.start(1)

    row_no = lax.broadcasted_iota(jnp.int32, (TOK, TOK), 0)
    col_no = lax.broadcasted_iota(jnp.int32, (TOK, TOK), 1)
    seg_row = jnp.broadcast_to(seg_ref[...], (TOK, TOK))
    seg_col = jnp.sum(jnp.where(row_no == col_no, seg_row, 0), axis=1, keepdims=True)
    earlier = jnp.sum((seg_row < seg_col).astype(F32), axis=1, keepdims=True)
    place = lax.broadcasted_iota(jnp.int32, (TOK, 1), 0).astype(F32)
    angle = (place - earlier) * freq_ref[...]
    cos_ref[...] = jnp.cos(angle)
    sin_ref[...] = jnp.sin(angle)
    mask_ref[...] = ((seg_row == seg_col) & (col_no <= row_no)).astype(F32)

    weights.wait(1)
    weights.start(2)

    def wait_x(k, carry):
        x_copy(k, lax.rem(d + k, N_DP)).wait_send()
        remote(
            xsend.at[d], xa.at[lax.rem(d + N_DP - k, N_DP)], x_s.at[k], x_r.at[k], d, t
        ).wait_recv()
        return carry

    lax.fori_loop(1, N_DP, wait_x, 0)
    for s, mask in enumerate(SLOTS):
        pair = [unfold(xa[xor_dp(d, mask ^ e)].astype(F32)) for e in range(2)]
        xg[rows_at(t * (N_DP * ROWS) + s * 2 * ROWS, 2 * ROWS, 16)] = jnp.concatenate(pair, axis=0).astype(BF16)
    tokens = Gather(xg, N_DP * ROWS, ((0, 128), (128, 128), (256, 128)), g_s, g_r, d, t)
    tokens.start(0)

    weights.wait(2)

    def project(n, carry):
        own = xg[rows_at(t * (N_DP * ROWS), N_DP * ROWS, 16)]
        kvf[:, rows_at(n * 256, 256, 256)] = dot_nt(own, wg[rows_at(n * 256, 256, 256)])
        return carry

    lax.fori_loop(0, 4, project, 0)

    def kv_copy(mask, to, slot):
        return remote(kvsend.at[mask], kvrecv.at[slot], kv_s.at[mask], kv_r.at[mask], to, t)

    for s, base in enumerate(SLOTS):
        for e in range(2):
            mask = base ^ e
            block = fold(kvf[(2 * s + e) * ROWS : (2 * s + e + 1) * ROWS]).astype(BF16)
            if mask == 0:
                kvrecv[0] = block
            else:
                kvsend[mask] = block
                kv_copy(mask, xor_dp(d, mask), mask).start()
    tokens.wait(0)
    tokens.start(1)
    for mask in range(1, N_DP):
        kv_copy(mask, xor_dp(d, mask), mask).wait()

    def add_kv(k, total):
        return total + kvrecv[k].astype(F32)

    lin = lax.fori_loop(1, N_DP, add_kv, kvrecv[0].astype(F32))
    for head in range(4):
        rows = lin[(head // 2) * ROWS : (head // 2 + 1) * ROWS, (head % 2) * 256 : (head % 2 + 1) * 256]
        heads_out[head] = jnp.concatenate([rows[:, :HD], rows[:, HD:]], axis=0).astype(BF16)

    def head_copy(k, to):
        return remote(heads_out.at[to // 2], heads_in.at[t], h_s.at[k], h_r.at[k], d, to)

    def send_heads(k, carry):
        head_copy(k, lax.rem(t + k, N_T)).start()
        return carry

    lax.fori_loop(1, N_T, send_heads, 0)
    heads_in[t] = heads_out[t // 2]
    tokens.wait(1)
    tokens.start(2)

    def wait_heads(k, carry):
        head_copy(k, lax.rem(t + k, N_T)).wait_send()
        slot = lax.rem(t + N_T - k, N_T)
        remote(heads_out.at[0], heads_in.at[slot], h_s.at[k], h_r.at[k], d, slot).wait_recv()
        return carry

    lax.fori_loop(1, N_T, wait_heads, 0)
    blocks = [heads_in[i].astype(F32) for i in range(N_T)]
    first = jnp.concatenate([b[:ROWS] for b in blocks], axis=0)
    second = jnp.concatenate([b[ROWS:] for b in blocks], axis=0)
    cosine, sine = cos_ref[...], sin_ref[...]
    a, c = first[:, :HALF], second[:, :HALF]
    key_ref[...] = jnp.concatenate([a * cosine - c * sine, c * cosine + a * sine], axis=1).astype(BF16)
    value_ref[...] = jnp.concatenate([first[:, HALF:], second[:, HALF:]], axis=1).astype(BF16)
    keyp[...] = jnp.zeros_like(keyp)
    valuep[...] = jnp.zeros_like(valuep)
    scale = 1.0 / HD**0.5

    def head_step(h, carry):
        cols = rows_at(h * HD, HD, HD)
        q, do = q_ref[:, cols], do_ref[:, cols]
        key, value = key_ref[...], value_ref[...]
        allowed = mask_ref[...] > 0.0
        weight = jnp.where(allowed, jnp.exp(dot_nt(q, key) * scale), 0.0)
        probs = weight / jnp.sum(weight, axis=1, keepdims=True)
        dprob = dot_nt(do, value)
        delta = jnp.sum(probs * dprob, axis=1, keepdims=True)
        dscore = (probs * (dprob - delta)).astype(BF16)
        gq_ref[:, cols] = (dot_nn(dscore, key) * scale).astype(BF16)
        keyp[...] += dot_tn(dscore, q)
        valuep[...] += dot_tn(probs.astype(BF16), do)
        return carry

    lax.fori_loop(0, COLS // HD, head_step, 0)
    key_part = keyp[...] * scale
    part_out[0:TOK] = key_part.astype(BF16)
    part_out[TOK : 2 * TOK] = valuep[...].astype(BF16)
    part = remote(part_out, part_in, p_s, p_r, d, xor_t(t, 1))
    part.start()
    part.wait()
    key_rot = key_part + part_in[0:TOK].astype(F32)
    value_sum = valuep[...] + part_in[TOK : 2 * TOK].astype(F32)
    upper, lower = key_rot[:, :HALF], key_rot[:, HALF:]
    is_first = lax.rem(t, 2) == 0
    own_key = jnp.where(is_first, upper * cosine + lower * sine, lower * cosine - upper * sine)
    own_value = jnp.where(is_first, value_sum[:, :HALF], value_sum[:, HALF:])
    own_ref[...] = jnp.concatenate([own_key, own_value], axis=1).astype(BF16)
    tokens.wait(2)
    weights.finish()
    tokens.finish()


def back(
    xg, gq_ref, own_ref, wq_ref, wk_ref, wv_ref,
    gr_ref, kw_ref, vw_ref, qw_ref,
    grads, xc, wkv, term, s1, k1, r1, s2, k2, r2, s3, k3, r3, done_out, done_in,
    d_s, d_r, f_s, f_r, e1_s, e1_r, e2_s, e2_r, e3_s, e3_r,
):
    d = lax.axis_index("dp")
    t = lax.axis_index("tensor")
    barrier = pltpu.get_barrier_semaphore()

    def greet_dp(k, carry):
        pl.semaphore_signal(barrier, inc=1, device_id=(lax.rem(d + k, N_DP), t), device_id_type=MESH)
        return carry

    lax.fori_loop(1, N_DP, greet_dp, 0)
    for link in (1, 2, 6):
        pl.semaphore_signal(barrier, inc=1, device_id=(d, xor_t(t, link)), device_id_type=MESH)
    grads[0:TOK, 0:COLS] = gq_ref[...]
    grads[0:TOK, COLS:WIDE] = own_ref[...]
    wkv[0:HALF] = wk_ref[...]
    wkv[HALF:HD] = wv_ref[...]
    pl.semaphore_wait(barrier, N_DP - 1 + 3)

    place = {}
    for s, mask in enumerate(SLOTS):
        place[mask], place[mask ^ 1] = 2 * s, 2 * s + 1

    def block_of(mask):
        return grads.at[pl.ds(place[mask] * TOK, TOK)]

    def grad_copy(mask, link):
        there = mask ^ link
        return remote(
            block_of(mask), block_of(there), d_s.at[place[there]], d_r.at[place[there]], xor_dp(d, link), t
        )

    def grad_arrival(mask):
        n = place[mask]
        return remote(block_of(mask), block_of(mask), d_s.at[n], d_r.at[n], xor_dp(d, 1), t)

    for link in (8, 2, 6, 1):
        grad_copy(0, link).start()
    onward = {8: (2, 6, 1), 2: (6, 1), 6: (1,), 10: (1,), 14: (2, 1), 4: (1,), 12: (1,)}

    def receive(mask):
        grad_arrival(mask).wait_recv()
        for link in onward.get(mask, ()):
            grad_copy(mask, link).start()

    def multiply(s):
        def part(n, carry):
            cols = rows_at(n * 256, 256, 256)
            own = grads[s * 2 * TOK : (s + 1) * 2 * TOK]
            total = dot_nt(own[:, :COLS], wq_ref[rows_at(n * 256, 256, 256)])
            term[:, cols] = total + dot_nn(own[:, COLS:], wkv[:, cols])
            return carry

        lax.fori_loop(0, 4, part, 0)

    def split(s):
        for e in range(2):
            for j in range(N_T):
                start = e * TOK + ROWS * xor_t(t, j)
                piece = fold(term[rows_at(start, ROWS, 8)]).astype(BF16)
                for o, (g1, g2, g3) in enumerate(ORDERS):
                    kept = [0, g3, g2, g2 ^ g3]
                    to, q = (k1, kept.index(j)) if j in kept else (s1, kept.index(j ^ g1))
                    row = q * 32 + e * 16
                    to[s, o, row : row + 16] = piece[o * 16 : o * 16 + 16]

    def hop(s, o, stage):
        src, dst, send, recv = (
            (s1, r1, e1_s, e1_r), (s2, r2, e2_s, e2_r), (s3, r3, e3_s, e3_r)
        )[stage]
        return remote(
            src.at[s, o], dst.at[s, o], send.at[s, o], recv.at[s, o], d, xor_t(t, ORDERS[o][stage])
        )

    def begin(s):
        split(s)
        for o in range(3):
            hop(s, o, 0).start()

    def second(s):
        for o in range(3):
            hop(s, o, 0).wait_recv()
            s2[s, o] = (k1[s, o, 64:].astype(F32) + r1[s, o, 64:].astype(F32)).astype(BF16)
            hop(s, o, 1).start()
            k2[s, o] = (k1[s, o, :64].astype(F32) + r1[s, o, :64].astype(F32)).astype(BF16)

    def third(s):
        for o in range(3):
            hop(s, o, 1).wait_recv()
            s3[s, o] = (k2[s, o, 32:].astype(F32) + r2[s, o, 32:].astype(F32)).astype(BF16)
            hop(s, o, 2).start()
            k3[s, o] = k2[s, o, :32].astype(F32) + r2[s, o, :32].astype(F32)

    def final_copy(n, mask):
        return remote(done_out.at[n], done_in.at[n], f_s.at[n], f_r.at[n], xor_dp(d, mask), t)

    def last(s):
        for o in range(3):
            hop(s, o, 2).wait_recv()
            total = (k3[s, o] + r3[s, o].astype(F32)).astype(BF16)
            for e in range(2):
                to = done_in if 2 * s + e == 0 else done_out
                to[2 * s + e, o * 16 : o * 16 + 16] = total[e * 16 : e * 16 + 16]
        for e in range(2):
            if 2 * s + e:
                final_copy(2 * s + e, SLOTS[s] ^ e).start()

    def reorder(i, carry):
        s, pair = i // 4, lax.rem(i, 4)
        one = xg[rows_at((2 * pair) * (N_DP * ROWS) + s * 2 * ROWS, 2 * ROWS, 16)].astype(F32)
        two = xg[rows_at((2 * pair + 1) * (N_DP * ROWS) + s * 2 * ROWS, 2 * ROWS, 16)].astype(F32)
        at = s * 2 * TOK + pair * 2 * ROWS
        xc[rows_at(at, 2 * ROWS, 16)] = jnp.concatenate([one[:ROWS], two[:ROWS]], axis=0).astype(BF16)
        xc[rows_at(at + TOK, 2 * ROWS, 16)] = jnp.concatenate([one[ROWS:], two[ROWS:]], axis=0).astype(BF16)
        return carry

    def weight_part(n):
        cols = slice(n * 256, (n + 1) * 256)
        qw_ref[cols] = dot_tn(xc[:, cols], grads[:, :COLS])

    steps = len(SLOTS)
    for s, mask in enumerate(SLOTS):
        if s == 1:
            lax.fori_loop(0, 32, reorder, 0)
            receive(8)
            receive(2)
            receive(6)
        if s == 4:
            receive(10)
            receive(14)
        if s >= 6:
            receive(mask)
        receive(mask ^ 1)
        multiply(s)
        begin(s)
        if s >= 1:
            second(s - 1)
        if s >= 2:
            third(s - 2)
        if s >= 3:
            last(s - 3)
    weight_part(0)
    second(steps - 1)
    third(steps - 2)
    last(steps - 3)
    weight_part(1)
    third(steps - 1)
    last(steps - 2)
    weight_part(2)
    last(steps - 1)
    weight_part(3)

    def pair_weights(n, carry):
        cols = rows_at(n * 256, 256, 256)
        total = dot_tn(grads[:, COLS:], xc[:, cols])
        kw_ref[:, cols] = total[:HALF]
        vw_ref[:, cols] = total[HALF:]
        return carry

    lax.fori_loop(0, 4, pair_weights, 0)
    for s, base in enumerate(SLOTS):
        for e in range(2):
            n, mask = 2 * s + e, base ^ e
            if n:
                final_copy(n, mask).wait()
            gr_ref[:, rows_at(xor_dp(d, mask) * FEAT, FEAT, FEAT)] = unfold(done_in[n].astype(F32)).astype(BF16)
            if n:
                grad_arrival(mask).wait_send()
        for o in range(3):
            for stage in range(3):
                hop(s, o, stage).wait_send()


def vmem(*shape, dtype=BF16):
    return pltpu.VMEM(shape, dtype)


def dma(*shape):
    return pltpu.SemaphoreType.DMA(shape)


def shards(x_rows, w_key, w_value, w_query, queries, grad_out, segment_ids):
    freqs = theta_base ** (-(2.0 * np.arange(HALF, dtype=np.float32)) / HD)
    freqs = jnp.asarray(freqs.astype(np.float32).reshape(1, HALF))
    in_vmem = pl.BlockSpec(memory_space=pltpu.VMEM)
    shape = jax.ShapeDtypeStruct
    key_t, value_t = w_key.T, w_value.T
    limit = 60 * 2**20
    gq, own, tokens = pl.pallas_call(
        front,
        out_shape=(shape((TOK, COLS), BF16), shape((TOK, HD), BF16), shape((N_DP * TOK, FEAT), BF16)),
        in_specs=[in_vmem] * 7,
        out_specs=(in_vmem,) * 3,
        scratch_shapes=[
            vmem(N_DP, 48, 512), vmem(N_DP, 48, 512), vmem(1024, FEAT), vmem(N_DP * ROWS, 1024, dtype=F32),
            vmem(N_DP, 48, 512), vmem(N_DP, 48, 512), vmem(4, 48, HD), vmem(N_T, 48, HD),
            vmem(2 * TOK, HD), vmem(2 * TOK, HD),
            vmem(TOK, HALF, dtype=F32), vmem(TOK, HALF, dtype=F32), vmem(TOK, TOK, dtype=F32),
            vmem(TOK, HD, dtype=F32), vmem(TOK, HD, dtype=F32), vmem(TOK, HD), vmem(TOK, HD),
            dma(N_DP), dma(N_DP), dma(3, 7), dma(3, 7), dma(3, 7), dma(3, 7),
            dma(N_DP), dma(N_DP), dma(N_T), dma(N_T), pltpu.SemaphoreType.DMA, pltpu.SemaphoreType.DMA,
        ],
        compiler_params=pltpu.CompilerParams(
            collective_id=0, has_side_effects=True, vmem_limit_bytes=limit
        ),
        name="front",
    )(x_rows, key_t, value_t, queries, grad_out, segment_ids, freqs)
    rows, key_w, value_w, query_w = pl.pallas_call(
        back,
        out_shape=(
            shape((ROWS, N_DP * FEAT), BF16), shape((HALF, FEAT), F32), shape((HALF, FEAT), F32),
            shape((FEAT, COLS), F32),
        ),
        in_specs=[in_vmem] * 6,
        out_specs=(in_vmem,) * 4,
        scratch_shapes=[
            vmem(N_DP * TOK, WIDE), vmem(N_DP * TOK, FEAT), vmem(HD, FEAT), vmem(2 * TOK, FEAT, dtype=F32),
            vmem(8, 3, 128, 512), vmem(8, 3, 128, 512), vmem(8, 3, 128, 512),
            vmem(8, 3, 64, 512), vmem(8, 3, 64, 512), vmem(8, 3, 64, 512),
            vmem(8, 3, 32, 512), vmem(8, 3, 32, 512, dtype=F32), vmem(8, 3, 32, 512),
            vmem(N_DP, 48, 512), vmem(N_DP, 48, 512),
            dma(N_DP), dma(N_DP), dma(N_DP), dma(N_DP),
            dma(8, 3), dma(8, 3), dma(8, 3), dma(8, 3), dma(8, 3), dma(8, 3),
        ],
        compiler_params=pltpu.CompilerParams(
            collective_id=1, has_side_effects=True, vmem_limit_bytes=limit
        ),
        name="back",
    )(tokens, gq, own, w_query, key_t, value_t)
    return (gq, rows, key_w.T, value_w.T, query_w)


def solution(mesh):
    placed = (
        P(("dp", "tensor"), None),
        P("dp", "tensor"),
        P("dp", "tensor"),
        P("dp", "tensor"),
        P("dp", "tensor"),
        P("dp", "tensor"),
        P("dp", None),
    )
    return jax.shard_map(
        shards,
        mesh=mesh,
        in_specs=placed,
        out_specs=(
            P("dp", "tensor"),
            P(("dp", "tensor"), None),
            P("dp", "tensor"),
            P("dp", "tensor"),
            P("dp", "tensor"),
        ),
        check_vma=False,
    )
```

```python
import jax
import jax.numpy as jnp
import numpy as np
from jax import lax
from jax.experimental import pallas as pl
from jax.experimental.pallas import tpu as pltpu
from jax.sharding import PartitionSpec as P

theta_base = 500000.0
MESH = pl.DeviceIdType.MESH
F32 = jnp.float32
BF16 = jnp.bfloat16

N_DP = 16
N_T = 8
ROWS = 24
TOK = 192
FEAT = 1024
COLS = 1024
HD = 128
HALF = 64
WIDE = COLS + HD
SLOTS = (0, 2, 6, 8, 10, 14, 4, 12)
REDUCE = (
    ((2, 6, 1), (6, 2, 1), (1, 2, 6)),
    ((2, 6, 1), (6, 2, 1), (6, 1, 2)),
    ((2, 6, 1), (6, 2, 1), (1, 6, 2)),
    ((2, 6, 1), (6, 2, 1), (2, 1, 6)),
)


def xor_ring(place, mask):
    if mask == 0:
        return place
    if mask == 1:
        return place + 1 - 2 * lax.rem(place, 2)
    if mask == 2:
        return lax.rem(place + 2, 4)
    return 3 - place


def xor_dp(d, mask):
    y_hi, z, core = d // 8, lax.rem(d // 2, 4), lax.rem(d, 2)
    y_hi = 1 - y_hi if mask & 8 else y_hi
    core = 1 - core if mask & 1 else core
    return y_hi * 8 + xor_ring(z, (mask // 2) % 4) * 2 + core


def xor_t(t, mask):
    x, y_lo = t // 2, lax.rem(t, 2)
    y_lo = 1 - y_lo if mask & 1 else y_lo
    return xor_ring(x, mask // 2) * 2 + y_lo


def rows_at(start, size, unit):
    return pl.ds(pl.multiple_of(start, unit), size)


def remote(src, dst, send, recv, d, t):
    return pltpu.make_async_remote_copy(
        src_ref=src, dst_ref=dst, send_sem=send, recv_sem=recv, device_id=(d, t), device_id_type=MESH
    )


def fold(block):
    return jnp.concatenate([block[:, : FEAT // 2], block[:, FEAT // 2 :]], axis=0)


def unfold(block):
    return jnp.concatenate([block[:ROWS], block[ROWS:]], axis=1)


def dot_nt(a, b):
    return lax.dot_general(a, b, (((1,), (1,)), ((), ())), preferred_element_type=F32)


def dot_nn(a, b):
    return lax.dot_general(a, b, (((1,), (0,)), ((), ())), preferred_element_type=F32)


def dot_tn(a, b):
    return lax.dot_general(a, b, (((0,), (0,)), ((), ())), preferred_element_type=F32)


class Gather:
    def __init__(self, buf, slot_rows, chunks, orders, send, recv, d, t):
        self.buf, self.slot_rows, self.chunks, self.orders = buf, slot_rows, chunks, orders
        self.send, self.recv, self.d, self.t = send, recv, d, t

    def copies(self, stage, arriving):
        out = []
        for c, (offset, size) in enumerate(self.chunks):
            first, second, third = self.orders[c]
            held = ([0], [0, first], [0, first, second, first ^ second])[stage]
            link = self.orders[c][stage]
            for j in held:
                slot = xor_t(self.t, j ^ link if arriving else j)
                part = self.buf.at[rows_at(slot * self.slot_rows + offset, size, 16)]
                n = (j ^ link) - 1
                out.append(
                    remote(part, part, self.send.at[c, n], self.recv.at[c, n], self.d, xor_t(self.t, link))
                )
        return out

    def start(self, stage):
        for copy in self.copies(stage, False):
            copy.start()

    def wait(self, stage):
        for copy in self.copies(stage, True):
            copy.wait_recv()

    def finish(self):
        for stage in range(3):
            for copy in self.copies(stage, False):
                copy.wait_send()


def kernel(
    x_ref, wk_ref, wv_ref, seg_ref, freq_ref, q_hbm, do_hbm, wq_hbm,
    gq_hbm, gr_ref, kw_ref, vw_ref, qw_hbm,
    q_ref, do_ref, wq_ref, qw_ref,
    xg, xsend, xa, wg, kvf, kvsend, kvrecv, heads_out, heads_in, part_out, part_in,
    cos_ref, sin_ref, mask_ref, keyp, valuep, key_ref, value_ref,
    grads, xc, term, s1, k1, r1, s2, k2, r2, s3, k3, r3, done_out, done_in,
    l_s, x_s, x_r, w_s, w_r, g_s, g_r, kv_s, kv_r, h_s, h_r, p_s, p_r,
    d_s, d_r, f_s, f_r, e1_s, e1_r, e2_s, e2_r, e3_s, e3_r,
):
    d = lax.axis_index("dp")
    t = lax.axis_index("tensor")
    barrier = pltpu.get_barrier_semaphore()

    def greet_dp(k, carry):
        pl.semaphore_signal(barrier, inc=1, device_id=(lax.rem(d + k, N_DP), t), device_id_type=MESH)
        return carry

    def greet_t(k, carry):
        pl.semaphore_signal(barrier, inc=1, device_id=(d, lax.rem(t + k, N_T)), device_id_type=MESH)
        return carry

    lax.fori_loop(1, N_DP, greet_dp, 0)
    lax.fori_loop(1, N_T, greet_t, 0)
    loads = [
        pltpu.make_async_copy(src, dst, l_s.at[n])
        for n, (src, dst) in enumerate(((q_hbm, q_ref), (do_hbm, do_ref), (wq_hbm, wq_ref)))
    ]
    for load in loads:
        load.start()
    wg[rows_at(t * HD, HALF, HALF)] = wk_ref[...]
    wg[rows_at(t * HD + HALF, HALF, HALF)] = wv_ref[...]
    pl.semaphore_wait(barrier, N_DP + N_T - 2)

    weights = Gather(wg, HD, ((0, 64), (64, 64)), ((1, 2, 6), (1, 6, 2)), w_s, w_r, d, t)
    weights.start(0)

    def x_copy(k, to):
        return remote(xsend.at[to], xa.at[d], x_s.at[k], x_r.at[k], to, t)

    def pack_x(k, carry):
        to = lax.rem(d + k, N_DP)
        block = x_ref[:, rows_at(to * FEAT, FEAT, FEAT)].astype(F32)
        xsend[to] = fold(block).astype(BF16)
        x_copy(k, to).start()
        return carry

    lax.fori_loop(1, N_DP, pack_x, 0)
    xa[d] = fold(x_ref[:, rows_at(d * FEAT, FEAT, FEAT)].astype(F32)).astype(BF16)
    weights.wait(0)
    weights.start(1)

    row_no = lax.broadcasted_iota(jnp.int32, (TOK, TOK), 0)
    col_no = lax.broadcasted_iota(jnp.int32, (TOK, TOK), 1)
    seg_row = jnp.broadcast_to(seg_ref[...], (TOK, TOK))
    seg_col = jnp.sum(jnp.where(row_no == col_no, seg_row, 0), axis=1, keepdims=True)
    earlier = jnp.sum((seg_row < seg_col).astype(F32), axis=1, keepdims=True)
    place = lax.broadcasted_iota(jnp.int32, (TOK, 1), 0).astype(F32)
    angle = (place - earlier) * freq_ref[...]
    cos_ref[...] = jnp.cos(angle)
    sin_ref[...] = jnp.sin(angle)
    mask_ref[...] = ((seg_row == seg_col) & (col_no <= row_no)).astype(F32)

    weights.wait(1)
    weights.start(2)

    def wait_x(k, carry):
        x_copy(k, lax.rem(d + k, N_DP)).wait_send()
        remote(
            xsend.at[d], xa.at[lax.rem(d + N_DP - k, N_DP)], x_s.at[k], x_r.at[k], d, t
        ).wait_recv()
        return carry

    lax.fori_loop(1, N_DP, wait_x, 0)
    for s, mask in enumerate(SLOTS):
        pair = [unfold(xa[xor_dp(d, mask ^ e)].astype(F32)) for e in range(2)]
        xg[rows_at(t * (N_DP * ROWS) + s * 2 * ROWS, 2 * ROWS, 16)] = jnp.concatenate(pair, axis=0).astype(BF16)
    tokens = Gather(
        xg, N_DP * ROWS, ((0, 160), (160, 80), (240, 144)), ((1, 2, 6), (2, 6, 1), (6, 1, 2)), g_s, g_r, d, t
    )
    tokens.start(0)

    weights.wait(2)

    def project(n, carry):
        own = xg[rows_at(t * (N_DP * ROWS), N_DP * ROWS, 16)]
        kvf[:, rows_at(n * 256, 256, 256)] = dot_nt(own, wg[rows_at(n * 256, 256, 256)])
        return carry

    lax.fori_loop(0, 4, project, 0)

    def kv_copy(mask):
        return remote(kvsend.at[mask], kvrecv.at[mask], kv_s.at[mask], kv_r.at[mask], xor_dp(d, mask), t)

    for s, base in enumerate(SLOTS):
        for e in range(2):
            mask = base ^ e
            block = fold(kvf[(2 * s + e) * ROWS : (2 * s + e + 1) * ROWS]).astype(BF16)
            if mask == 0:
                kvrecv[0] = block
            else:
                kvsend[mask] = block
                kv_copy(mask).start()
    tokens.wait(0)
    tokens.start(1)
    for mask in range(1, N_DP):
        kv_copy(mask).wait()

    def add_kv(k, total):
        return total + kvrecv[k].astype(F32)

    lin = lax.fori_loop(1, N_DP, add_kv, kvrecv[0].astype(F32))
    for head in range(4):
        rows = lin[(head // 2) * ROWS : (head // 2 + 1) * ROWS, (head % 2) * 256 : (head % 2 + 1) * 256]
        heads_out[head] = jnp.concatenate([rows[:, :HD], rows[:, HD:]], axis=0).astype(BF16)

    def head_copy(k, to):
        return remote(heads_out.at[to // 2], heads_in.at[t], h_s.at[k], h_r.at[k], d, to)

    def send_heads(k, carry):
        head_copy(k, lax.rem(t + k, N_T)).start()
        return carry

    lax.fori_loop(1, N_T, send_heads, 0)
    heads_in[t] = heads_out[t // 2]

    def wait_heads(k, carry):
        head_copy(k, lax.rem(t + k, N_T)).wait_send()
        slot = lax.rem(t + N_T - k, N_T)
        remote(heads_out.at[0], heads_in.at[slot], h_s.at[k], h_r.at[k], d, slot).wait_recv()
        return carry

    lax.fori_loop(1, N_T, wait_heads, 0)
    tokens.wait(1)
    tokens.start(2)
    blocks = [heads_in[i].astype(F32) for i in range(N_T)]
    first = jnp.concatenate([b[:ROWS] for b in blocks], axis=0)
    second_part = jnp.concatenate([b[ROWS:] for b in blocks], axis=0)
    cosine, sine = cos_ref[...], sin_ref[...]
    a, c = first[:, :HALF], second_part[:, :HALF]
    key_ref[...] = jnp.concatenate([a * cosine - c * sine, c * cosine + a * sine], axis=1).astype(BF16)
    value_ref[...] = jnp.concatenate([first[:, HALF:], second_part[:, HALF:]], axis=1).astype(BF16)
    keyp[...] = jnp.zeros_like(keyp)
    valuep[...] = jnp.zeros_like(valuep)
    scale = 1.0 / HD**0.5
    for load in loads:
        load.wait()

    def head_step(h, carry):
        cols = rows_at(h * HD, HD, HD)
        q, do = q_ref[:, cols], do_ref[:, cols]
        key, value = key_ref[...], value_ref[...]
        allowed = mask_ref[...] > 0.0
        weight = jnp.where(allowed, jnp.exp(dot_nt(q, key) * scale), 0.0)
        probs = weight / jnp.sum(weight, axis=1, keepdims=True)
        dprob = dot_nt(do, value)
        delta = jnp.sum(probs * dprob, axis=1, keepdims=True)
        dscore = (probs * (dprob - delta)).astype(BF16)
        grads[0:TOK, cols] = (dot_nn(dscore, key) * scale).astype(BF16)
        keyp[...] += dot_tn(dscore, q)
        valuep[...] += dot_tn(probs.astype(BF16), do)
        return carry

    lax.fori_loop(0, COLS // HD, head_step, 0)
    key_part = keyp[...] * scale
    part_out[0:TOK] = key_part.astype(BF16)
    part_out[TOK : 2 * TOK] = valuep[...].astype(BF16)
    part = remote(part_out, part_in, p_s, p_r, d, xor_t(t, 1))
    part.start()
    part.wait()
    key_rot = key_part + part_in[0:TOK].astype(F32)
    value_sum = valuep[...] + part_in[TOK : 2 * TOK].astype(F32)
    upper, lower = key_rot[:, :HALF], key_rot[:, HALF:]
    is_first = lax.rem(t, 2) == 0
    own_key = jnp.where(is_first, upper * cosine + lower * sine, lower * cosine - upper * sine)
    own_value = jnp.where(is_first, value_sum[:, :HALF], value_sum[:, HALF:])
    grads[0:TOK, COLS:WIDE] = jnp.concatenate([own_key, own_value], axis=1).astype(BF16)

    place = {}
    for s, mask in enumerate(SLOTS):
        place[mask], place[mask ^ 1] = 2 * s, 2 * s + 1

    def block_of(mask):
        return grads.at[pl.ds(place[mask] * TOK, TOK)]

    def grad_copy(mask, link):
        there = mask ^ link
        return remote(
            block_of(mask), block_of(there), d_s.at[place[there]], d_r.at[place[there]], xor_dp(d, link), t
        )

    def grad_arrival(mask):
        n = place[mask]
        return remote(block_of(mask), block_of(mask), d_s.at[n], d_r.at[n], xor_dp(d, 1), t)

    for link in (8, 2, 6, 1):
        grad_copy(0, link).start()
    gq_out = pltpu.make_async_copy(grads.at[0:TOK, 0:COLS], gq_hbm, l_s.at[3])
    gq_out.start()
    onward = {8: (2, 6, 1), 2: (6, 1), 6: (1,), 10: (1,), 14: (2, 1), 4: (1,), 12: (1,)}

    def receive(*masks):
        for mask in masks:
            grad_arrival(mask).wait_recv()
            for link in onward.get(mask, ()):
                grad_copy(mask, link).start()

    def multiply(s):
        def part(n, carry):
            cols = rows_at(n * 256, 256, 256)
            own = grads[s * 2 * TOK : (s + 1) * 2 * TOK]
            total = dot_nt(own[:, :COLS], wq_ref[rows_at(n * 256, 256, 256)])
            term[:, cols] = total + dot_nn(own[:, COLS:], wg[rows_at(t * HD, HD, HD), cols])
            return carry

        lax.fori_loop(0, 4, part, 0)

    def split(s):
        for e in range(2):
            for j in range(N_T):
                start = e * TOK + ROWS * xor_t(t, j)
                piece = fold(term[rows_at(start, ROWS, 8)]).astype(BF16)
                for o, (g1, g2, g3) in enumerate(REDUCE[s % 4]):
                    kept = [0, g3, g2, g2 ^ g3]
                    to, q = (k1, kept.index(j)) if j in kept else (s1, kept.index(j ^ g1))
                    row = q * 32 + e * 16
                    to[s, o, row : row + 16] = piece[o * 16 : o * 16 + 16]

    def hop(s, o, stage):
        src, dst, send, recv = (
            (s1, r1, e1_s, e1_r), (s2, r2, e2_s, e2_r), (s3, r3, e3_s, e3_r)
        )[stage]
        return remote(
            src.at[s, o], dst.at[s, o], send.at[s, o], recv.at[s, o], d, xor_t(t, REDUCE[s % 4][o][stage])
        )

    def begin(s):
        multiply(s)
        split(s)
        for o in range(3):
            hop(s, o, 0).start()

    def second(s):
        for o in range(3):
            hop(s, o, 0).wait_recv()
            s2[s, o] = (k1[s, o, 64:].astype(F32) + r1[s, o, 64:].astype(F32)).astype(BF16)
            hop(s, o, 1).start()
            k2[s, o] = (k1[s, o, :64].astype(F32) + r1[s, o, :64].astype(F32)).astype(BF16)

    def third(s):
        for o in range(3):
            hop(s, o, 1).wait_recv()
            s3[s, o] = (k2[s, o, 32:].astype(F32) + r2[s, o, 32:].astype(F32)).astype(BF16)
            hop(s, o, 2).start()
            k3[s, o] = k2[s, o, :32].astype(F32) + r2[s, o, :32].astype(F32)

    def final_copy(n, mask):
        return remote(done_out.at[n], done_in.at[n], f_s.at[n], f_r.at[n], xor_dp(d, mask), t)

    def last(s):
        for o in range(3):
            hop(s, o, 2).wait_recv()
            total = (k3[s, o] + r3[s, o].astype(F32)).astype(BF16)
            for e in range(2):
                to = done_in if 2 * s + e == 0 else done_out
                to[2 * s + e, o * 16 : o * 16 + 16] = total[e * 16 : e * 16 + 16]
        for e in range(2):
            if 2 * s + e:
                final_copy(2 * s + e, SLOTS[s] ^ e).start()

    def reorder(i, carry):
        s, pair = i // 4, lax.rem(i, 4)
        one = xg[rows_at((2 * pair) * (N_DP * ROWS) + s * 2 * ROWS, 2 * ROWS, 16)].astype(F32)
        two = xg[rows_at((2 * pair + 1) * (N_DP * ROWS) + s * 2 * ROWS, 2 * ROWS, 16)].astype(F32)
        at = s * 2 * TOK + pair * 2 * ROWS
        xc[rows_at(at, 2 * ROWS, 16)] = jnp.concatenate([one[:ROWS], two[:ROWS]], axis=0).astype(BF16)
        xc[rows_at(at + TOK, 2 * ROWS, 16)] = jnp.concatenate([one[ROWS:], two[ROWS:]], axis=0).astype(BF16)
        return carry

    def weight_copy(n):
        rows = pl.ds(n * 256, 256)
        return pltpu.make_async_copy(qw_ref.at[rows], qw_hbm.at[rows], l_s.at[4 + n])

    def weight_part(n):
        cols = slice(n * 256, (n + 1) * 256)
        qw_ref[cols] = dot_tn(xc[:, cols], grads[:, :COLS])
        weight_copy(n).start()

    def pair_weights(n, carry):
        cols = rows_at(n * 256, 256, 256)
        total = dot_tn(grads[:, COLS:], xc[:, cols])
        kw_ref[:, cols] = total[:HALF]
        vw_ref[:, cols] = total[HALF:]
        return carry

    receive(1)
    begin(0)
    receive(8, 2, 6)
    second(0)
    receive(3)
    begin(1)
    third(0)
    receive(7)
    begin(2)
    second(1)
    receive(9)
    begin(3)
    last(0)
    second(2)
    third(1)
    receive(10, 14)
    second(3)
    receive(11)
    begin(4)
    third(2)
    last(1)
    receive(15)
    begin(5)
    tokens.wait(2)
    lax.fori_loop(0, 32, reorder, 0)
    second(4)
    third(3)
    last(2)
    receive(4, 12, 5)
    begin(6)
    second(5)
    third(4)
    last(3)
    receive(13)
    begin(7)
    weight_part(0)
    second(6)
    third(5)
    last(4)
    weight_part(1)
    second(7)
    third(6)
    last(5)
    weight_part(2)
    third(7)
    last(6)
    weight_part(3)
    last(7)
    lax.fori_loop(0, 4, pair_weights, 0)
    for s, base in enumerate(SLOTS):
        for e in range(2):
            n, mask = 2 * s + e, base ^ e
            if n:
                final_copy(n, mask).wait()
            gr_ref[:, rows_at(xor_dp(d, mask) * FEAT, FEAT, FEAT)] = unfold(done_in[n].astype(F32)).astype(BF16)
            if n:
                grad_arrival(mask).wait_send()
        for o in range(3):
            for stage in range(3):
                hop(s, o, stage).wait_send()
    weights.finish()
    tokens.finish()
    gq_out.wait()
    for n in range(4):
        weight_copy(n).wait()


def emit(*refs):
    count = len(refs) // 2
    sems = refs[-1]
    copies = []
    for src, dst in zip(refs[:count], refs[count : 2 * count]):
        parts = 4 if src.shape[0] >= FEAT else 1
        size = src.shape[0] // parts
        for n in range(parts):
            rows = pl.ds(n * size, size)
            copies.append(pltpu.make_async_copy(src.at[rows], dst.at[rows], sems.at[len(copies)]))
    for copy in copies:
        copy.start()
    for copy in copies:
        copy.wait()


def vmem(*shape, dtype=BF16):
    return pltpu.VMEM(shape, dtype)


def dma(*shape):
    return pltpu.SemaphoreType.DMA(shape)


def shards(x_rows, w_key, w_value, w_query, queries, grad_out, segment_ids):
    freqs = theta_base ** (-(2.0 * np.arange(HALF, dtype=np.float32)) / HD)
    freqs = jnp.asarray(freqs.astype(np.float32).reshape(1, HALF))
    in_vmem = pl.BlockSpec(memory_space=pltpu.VMEM)
    anywhere = pl.BlockSpec(memory_space=pl.ANY)
    shape = jax.ShapeDtypeStruct
    results = (
        shape((TOK, COLS), BF16), shape((ROWS, N_DP * FEAT), BF16), shape((HALF, FEAT), F32),
        shape((HALF, FEAT), F32), shape((FEAT, COLS), F32),
    )
    outs = pl.pallas_call(
        kernel,
        out_shape=results,
        in_specs=[in_vmem] * 5 + [anywhere] * 3,
        out_specs=(anywhere, in_vmem, in_vmem, in_vmem, anywhere),
        scratch_shapes=[
            vmem(TOK, COLS), vmem(TOK, COLS), vmem(FEAT, COLS), vmem(FEAT, COLS, dtype=F32),
            vmem(N_DP * TOK, FEAT), vmem(N_DP, 48, 512), vmem(N_DP, 48, 512), vmem(1024, FEAT),
            vmem(N_DP * ROWS, 1024, dtype=F32), vmem(N_DP, 48, 512), vmem(N_DP, 48, 512),
            vmem(4, 48, HD), vmem(N_T, 48, HD), vmem(2 * TOK, HD), vmem(2 * TOK, HD),
            vmem(TOK, HALF, dtype=F32), vmem(TOK, HALF, dtype=F32), vmem(TOK, TOK, dtype=F32),
            vmem(TOK, HD, dtype=F32), vmem(TOK, HD, dtype=F32), vmem(TOK, HD), vmem(TOK, HD),
            vmem(N_DP * TOK, WIDE), vmem(N_DP * TOK, FEAT), vmem(2 * TOK, FEAT, dtype=F32),
            vmem(8, 3, 128, 512), vmem(8, 3, 128, 512), vmem(8, 3, 128, 512),
            vmem(8, 3, 64, 512), vmem(8, 3, 64, 512), vmem(8, 3, 64, 512),
            vmem(8, 3, 32, 512), vmem(8, 3, 32, 512, dtype=F32), vmem(8, 3, 32, 512),
            vmem(N_DP, 48, 512), vmem(N_DP, 48, 512),
            dma(8), dma(N_DP), dma(N_DP), dma(2, 7), dma(2, 7), dma(3, 7), dma(3, 7),
            dma(N_DP), dma(N_DP), dma(N_T), dma(N_T), pltpu.SemaphoreType.DMA, pltpu.SemaphoreType.DMA,
            dma(N_DP), dma(N_DP), dma(N_DP), dma(N_DP),
            dma(8, 3), dma(8, 3), dma(8, 3), dma(8, 3), dma(8, 3), dma(8, 3),
        ],
        compiler_params=pltpu.CompilerParams(
            collective_id=0, has_side_effects=True, vmem_limit_bytes=62 * 2**20
        ),
        name="grads",
    )(x_rows, w_key.T, w_value.T, segment_ids, freqs, queries, grad_out, w_query)
    gq, rows, key_w, value_w, query_w = pl.pallas_call(
        emit,
        out_shape=results,
        in_specs=[anywhere] * 5,
        out_specs=(anywhere,) * 5,
        scratch_shapes=[dma(8)],
        name="emit",
    )(*outs)
    return (gq, rows, key_w.T, value_w.T, query_w)


def solution(mesh):
    placed = (
        P(("dp", "tensor"), None),
        P("dp", "tensor"),
        P("dp", "tensor"),
        P("dp", "tensor"),
        P("dp", "tensor"),
        P("dp", "tensor"),
        P("dp", None),
    )
    return jax.shard_map(
        shards,
        mesh=mesh,
        in_specs=placed,
        out_specs=(
            P("dp", "tensor"),
            P(("dp", "tensor"), None),
            P("dp", "tensor"),
            P("dp", "tensor"),
            P("dp", "tensor"),
        ),
        check_vma=False,
    )
```

```python
import jax
import jax.numpy as jnp
import numpy as np
from jax import lax
from jax.experimental import pallas as pl
from jax.experimental.pallas import tpu as pltpu
from jax.sharding import PartitionSpec as P

theta_base = 500000.0
MESH = pl.DeviceIdType.MESH
F32 = jnp.float32
BF16 = jnp.bfloat16

N_DP = 16
N_T = 8
ROWS = 24
TOK = 192
FEAT = 1024
COLS = 1024
HD = 128
HALF = 64
WIDE = COLS + HD
SLOTS = (0, 2, 6, 8, 10, 14, 4, 12)
ORDERS = ((1, 2, 6), (2, 6, 1), (6, 1, 2))


def xor_ring(place, mask):
    if mask == 0:
        return place
    if mask == 1:
        return place + 1 - 2 * lax.rem(place, 2)
    if mask == 2:
        return lax.rem(place + 2, 4)
    return 3 - place


def xor_dp(d, mask):
    y_hi, z, core = d // 8, lax.rem(d // 2, 4), lax.rem(d, 2)
    y_hi = 1 - y_hi if mask & 8 else y_hi
    core = 1 - core if mask & 1 else core
    return y_hi * 8 + xor_ring(z, (mask // 2) % 4) * 2 + core


def xor_t(t, mask):
    x, y_lo = t // 2, lax.rem(t, 2)
    y_lo = 1 - y_lo if mask & 1 else y_lo
    return xor_ring(x, mask // 2) * 2 + y_lo


def rows_at(start, size, unit):
    return pl.ds(pl.multiple_of(start, unit), size)


def remote(src, dst, send, recv, d, t):
    return pltpu.make_async_remote_copy(
        src_ref=src, dst_ref=dst, send_sem=send, recv_sem=recv, device_id=(d, t), device_id_type=MESH
    )


def fold(block):
    return jnp.concatenate([block[:, : FEAT // 2], block[:, FEAT // 2 :]], axis=0)


def unfold(block):
    return jnp.concatenate([block[:ROWS], block[ROWS:]], axis=1)


def dot_nt(a, b):
    return lax.dot_general(a, b, (((1,), (1,)), ((), ())), preferred_element_type=F32)


def dot_nn(a, b):
    return lax.dot_general(a, b, (((1,), (0,)), ((), ())), preferred_element_type=F32)


def dot_tn(a, b):
    return lax.dot_general(a, b, (((0,), (0,)), ((), ())), preferred_element_type=F32)


class Gather:
    def __init__(self, buf, slot_rows, chunks, orders, send, recv, d, t):
        self.buf, self.slot_rows, self.chunks, self.orders = buf, slot_rows, chunks, orders
        self.send, self.recv, self.d, self.t = send, recv, d, t

    def copies(self, stage, arriving, only=(1, 2, 0)):
        out = []
        for c in only:
            offset, size = self.chunks[c]
            first, second, third = self.orders[c]
            held = ([0], [0, first], [0, first, second, first ^ second])[stage]
            link = self.orders[c][stage]
            for j in held:
                slot = xor_t(self.t, j ^ link if arriving else j)
                part = self.buf.at[rows_at(slot * self.slot_rows + offset, size, 16)]
                n = (j ^ link) - 1
                out.append(
                    remote(part, part, self.send.at[c, n], self.recv.at[c, n], self.d, xor_t(self.t, link))
                )
        return out

    def start(self, stage):
        for copy in self.copies(stage, False):
            copy.start()

    def wait(self, stage):
        for copy in self.copies(stage, True):
            copy.wait_recv()

    def step(self, stage):
        for c in (1, 2, 0):
            for copy in self.copies(stage, True, (c,)):
                copy.wait_recv()
            for copy in self.copies(stage + 1, False, (c,)):
                copy.start()

    def finish(self):
        for stage in range(3):
            for copy in self.copies(stage, False):
                copy.wait_send()


def kernel(
    x_ref, wk_ref, wv_ref, seg_ref, freq_ref, q_hbm, do_hbm, wq_hbm,
    gq_hbm, gr_ref, kw_ref, vw_ref, qw_hbm,
    q_ref, do_ref, wq_ref, qw_ref,
    xg, xa, wg, kvf, kvsend, kvswap, kvrecv, heads_out, heads_in, part_out, part_in,
    cos_ref, sin_ref, mask_ref, keyp, valuep, key_ref, value_ref,
    grads, xc, term, s1, k1, r1, s2, k2, r2, s3, k3, r3, done_out, done_in,
    l_s, x_s, x_r, w_s, w_r, g_s, g_r, kv_s, kv_r, h_s, h_r, p_s, p_r,
    d_s, d_r, f_s, f_r, e1_s, e1_r, e2_s, e2_r, e3_s, e3_r,
):
    d = lax.axis_index("dp")
    t = lax.axis_index("tensor")
    barrier = pltpu.get_barrier_semaphore()

    def greet_dp(k, carry):
        pl.semaphore_signal(barrier, inc=1, device_id=(lax.rem(d + k, N_DP), t), device_id_type=MESH)
        return carry

    def greet_t(k, carry):
        pl.semaphore_signal(barrier, inc=1, device_id=(d, lax.rem(t + k, N_T)), device_id_type=MESH)
        return carry

    lax.fori_loop(1, N_DP, greet_dp, 0)
    lax.fori_loop(1, N_T, greet_t, 0)
    loads = [
        pltpu.make_async_copy(src, dst, l_s.at[n])
        for n, (src, dst) in enumerate(((q_hbm, q_ref), (do_hbm, do_ref), (wq_hbm, wq_ref)))
    ]
    for load in loads:
        load.start()
    wg[rows_at(t * HD, HALF, HALF)] = wk_ref[...]
    wg[rows_at(t * HD + HALF, HALF, HALF)] = wv_ref[...]
    pl.semaphore_wait(barrier, N_DP + N_T - 2)

    weights = Gather(wg, HD, ((0, 48), (48, 32), (80, 48)), ORDERS, w_s, w_r, d, t)
    weights.start(0)

    def x_copy(k):
        to = lax.rem(d + k, N_DP)
        return remote(
            x_ref.at[:, rows_at(to * FEAT, FEAT, FEAT)], xa.at[d], x_s.at[k], x_r.at[k], to, t
        )

    def send_x(k, carry):
        x_copy(k).start()
        return carry

    lax.fori_loop(1, N_DP, send_x, 0)
    weights.step(0)
    weights.step(1)
    xa[d] = x_ref[:, rows_at(d * FEAT, FEAT, FEAT)]

    row_no = lax.broadcasted_iota(jnp.int32, (TOK, TOK), 0)
    col_no = lax.broadcasted_iota(jnp.int32, (TOK, TOK), 1)
    seg_row = jnp.broadcast_to(seg_ref[...], (TOK, TOK))
    seg_col = jnp.sum(jnp.where(row_no == col_no, seg_row, 0), axis=1, keepdims=True)
    earlier = jnp.sum((seg_row < seg_col).astype(F32), axis=1, keepdims=True)
    place = lax.broadcasted_iota(jnp.int32, (TOK, 1), 0).astype(F32)
    angle = (place - earlier) * freq_ref[...]
    cos_ref[...] = jnp.cos(angle)
    sin_ref[...] = jnp.sin(angle)
    mask_ref[...] = ((seg_row == seg_col) & (col_no <= row_no)).astype(F32)

    def wait_x(k, carry):
        x_copy(k).wait_send()
        slot = xa.at[lax.rem(d + N_DP - k, N_DP)]
        remote(slot, slot, x_s.at[k], x_r.at[k], d, t).wait_recv()
        return carry

    lax.fori_loop(1, N_DP, wait_x, 0)
    for s, mask in enumerate(SLOTS):
        pair = [xa[xor_dp(d, mask ^ e)].astype(F32) for e in range(2)]
        xg[rows_at(t * (N_DP * ROWS) + s * 2 * ROWS, 2 * ROWS, 16)] = jnp.concatenate(pair, axis=0).astype(BF16)
    tokens = Gather(
        xg, N_DP * ROWS, ((0, 160), (160, 80), (240, 144)), ORDERS, g_s, g_r, d, t
    )
    tokens.start(0)

    weights.wait(2)

    def project(n, carry):
        own = xg[rows_at(t * (N_DP * ROWS), N_DP * ROWS, 16)]
        kvf[:, rows_at(n * 256, 256, 256)] = dot_nt(own, wg[rows_at(n * 256, 256, 256)])
        return carry

    lax.fori_loop(0, 4, project, 0)

    swap = remote(kvsend.at[1], kvswap, kv_s.at[0], kv_r.at[0], xor_dp(d, 1), t)

    def kv_copy(s):
        return remote(
            kvsend.at[0, s], kvrecv.at[s], kv_s.at[s], kv_r.at[s], xor_dp(d, SLOTS[s]), t
        )

    def kv_part(n):
        return fold(kvf[n * ROWS : (n + 1) * ROWS])

    for s in range(len(SLOTS)):
        kvsend[1, s] = kv_part(2 * s + 1).astype(BF16)
    swap.start()
    swap.wait()
    for s in range(1, len(SLOTS)):
        kvsend[0, s] = (kv_part(2 * s) + kvswap[s].astype(F32)).astype(BF16)
        kv_copy(s).start()
    tokens.step(0)
    lin = kv_part(0) + kvswap[0].astype(F32)
    for s in range(1, len(SLOTS)):
        kv_copy(s).wait()
        lin = lin + kvrecv[s].astype(F32)
    for head in range(4):
        rows = lin[(head // 2) * ROWS : (head // 2 + 1) * ROWS, (head % 2) * 256 : (head % 2 + 1) * 256]
        heads_out[head] = jnp.concatenate([rows[:, :HD], rows[:, HD:]], axis=0).astype(BF16)

    def head_copy(k, to):
        return remote(heads_out.at[to // 2], heads_in.at[t], h_s.at[k], h_r.at[k], d, to)

    def send_heads(k, carry):
        head_copy(k, lax.rem(t + k, N_T)).start()
        return carry

    lax.fori_loop(1, N_T, send_heads, 0)
    heads_in[t] = heads_out[t // 2]

    def wait_heads(k, carry):
        head_copy(k, lax.rem(t + k, N_T)).wait_send()
        slot = lax.rem(t + N_T - k, N_T)
        remote(heads_out.at[0], heads_in.at[slot], h_s.at[k], h_r.at[k], d, slot).wait_recv()
        return carry

    lax.fori_loop(1, N_T, wait_heads, 0)
    tokens.step(1)
    blocks = [heads_in[i].astype(F32) for i in range(N_T)]
    first = jnp.concatenate([b[:ROWS] for b in blocks], axis=0)
    second_part = jnp.concatenate([b[ROWS:] for b in blocks], axis=0)
    cosine, sine = cos_ref[...], sin_ref[...]
    a, c = first[:, :HALF], second_part[:, :HALF]
    key_ref[...] = jnp.concatenate([a * cosine - c * sine, c * cosine + a * sine], axis=1).astype(BF16)
    value_ref[...] = jnp.concatenate([first[:, HALF:], second_part[:, HALF:]], axis=1).astype(BF16)
    keyp[...] = jnp.zeros_like(keyp)
    valuep[...] = jnp.zeros_like(valuep)
    scale = 1.0 / HD**0.5
    for load in loads:
        load.wait()

    def head_step(h, carry):
        cols = rows_at(h * HD, HD, HD)
        q, do = q_ref[:, cols], do_ref[:, cols]
        key, value = key_ref[...], value_ref[...]
        allowed = mask_ref[...] > 0.0
        weight = jnp.where(allowed, jnp.exp(dot_nt(q, key) * scale), 0.0)
        probs = weight / jnp.sum(weight, axis=1, keepdims=True)
        dprob = dot_nt(do, value)
        delta = jnp.sum(probs * dprob, axis=1, keepdims=True)
        dscore = (probs * (dprob - delta)).astype(BF16)
        grads[0:TOK, cols] = (dot_nn(dscore, key) * scale).astype(BF16)
        keyp[...] += dot_tn(dscore, q)
        valuep[...] += dot_tn(probs.astype(BF16), do)
        return carry

    lax.fori_loop(0, COLS // HD, head_step, 0)
    key_part = keyp[...] * scale
    part_out[0:TOK] = key_part.astype(BF16)
    part_out[TOK : 2 * TOK] = valuep[...].astype(BF16)
    part = remote(part_out, part_in, p_s, p_r, d, xor_t(t, 1))
    part.start()
    part.wait()
    key_rot = key_part + part_in[0:TOK].astype(F32)
    value_sum = valuep[...] + part_in[TOK : 2 * TOK].astype(F32)
    upper, lower = key_rot[:, :HALF], key_rot[:, HALF:]
    is_first = lax.rem(t, 2) == 0
    own_key = jnp.where(is_first, upper * cosine + lower * sine, lower * cosine - upper * sine)
    own_value = jnp.where(is_first, value_sum[:, :HALF], value_sum[:, HALF:])
    grads[0:TOK, COLS:WIDE] = jnp.concatenate([own_key, own_value], axis=1).astype(BF16)

    place = {}
    for s, mask in enumerate(SLOTS):
        place[mask], place[mask ^ 1] = 2 * s, 2 * s + 1

    def block_of(mask):
        return grads.at[pl.ds(place[mask] * TOK, TOK)]

    def grad_copy(mask, link):
        there = mask ^ link
        return remote(
            block_of(mask), block_of(there), d_s.at[place[there]], d_r.at[place[there]], xor_dp(d, link), t
        )

    def grad_arrival(mask):
        n = place[mask]
        return remote(block_of(mask), block_of(mask), d_s.at[n], d_r.at[n], xor_dp(d, 1), t)

    for link in (8, 2, 6, 1):
        grad_copy(0, link).start()
    gq_out = pltpu.make_async_copy(grads.at[0:TOK, 0:COLS], gq_hbm, l_s.at[3])
    gq_out.start()
    onward = {8: (2, 6, 1), 2: (1,), 6: (1,), 10: (1,), 14: (2, 1), 4: (1,), 12: (1,)}

    def receive(*masks):
        for mask in masks:
            grad_arrival(mask).wait_recv()
            for link in onward.get(mask, ()):
                grad_copy(mask, link).start()
            if mask == 14:
                grad_copy(2, 6).start()

    def multiply(s):
        def part(n, carry):
            cols = rows_at(n * 256, 256, 256)
            own = grads[s * 2 * TOK : (s + 1) * 2 * TOK]
            total = dot_nt(own[:, :COLS], wq_ref[rows_at(n * 256, 256, 256)])
            term[:, cols] = total + dot_nn(own[:, COLS:], wg[rows_at(t * HD, HD, HD), cols])
            return carry

        lax.fori_loop(0, 4, part, 0)

    def split(s):
        for e in range(2):
            for j in range(N_T):
                start = e * TOK + ROWS * xor_t(t, j)
                piece = fold(term[rows_at(start, ROWS, 8)]).astype(BF16)
                for o, (g1, g2, g3) in enumerate(ORDERS):
                    kept = [0, g3, g2, g2 ^ g3]
                    to, q = (k1, kept.index(j)) if j in kept else (s1, kept.index(j ^ g1))
                    row = q * 32 + e * 16
                    to[s, o, row : row + 16] = piece[o * 16 : o * 16 + 16]

    def hop(s, o, stage):
        src, dst, send, recv = (
            (s1, r1, e1_s, e1_r), (s2, r2, e2_s, e2_r), (s3, r3, e3_s, e3_r)
        )[stage]
        return remote(
            src.at[s, o], dst.at[s, o], send.at[s, o], recv.at[s, o], d, xor_t(t, ORDERS[o][stage])
        )

    def begin(s):
        multiply(s)
        split(s)
        for o in range(3):
            hop(s, o, 0).start()

    def second(s):
        for o in range(3):
            hop(s, o, 0).wait_recv()
            s2[s, o] = (k1[s, o, 64:].astype(F32) + r1[s, o, 64:].astype(F32)).astype(BF16)
            hop(s, o, 1).start()
            k2[s, o] = (k1[s, o, :64].astype(F32) + r1[s, o, :64].astype(F32)).astype(BF16)

    def third(s):
        for o in range(3):
            hop(s, o, 1).wait_recv()
            s3[s, o] = (k2[s, o, 32:].astype(F32) + r2[s, o, 32:].astype(F32)).astype(BF16)
            hop(s, o, 2).start()
            k3[s, o] = k2[s, o, :32].astype(F32) + r2[s, o, :32].astype(F32)

    def final_copy(n, mask):
        return remote(done_out.at[n], done_in.at[n], f_s.at[n], f_r.at[n], xor_dp(d, mask), t)

    def last(s):
        for o in range(3):
            hop(s, o, 2).wait_recv()
            total = (k3[s, o] + r3[s, o].astype(F32)).astype(BF16)
            for e in range(2):
                to = done_in if 2 * s + e == 0 else done_out
                to[2 * s + e, o * 16 : o * 16 + 16] = total[e * 16 : e * 16 + 16]
        for e in range(2):
            if 2 * s + e:
                final_copy(2 * s + e, SLOTS[s] ^ e).start()

    def reorder(i, carry):
        s, pair = i // 4, lax.rem(i, 4)
        one = xg[rows_at((2 * pair) * (N_DP * ROWS) + s * 2 * ROWS, 2 * ROWS, 16)].astype(F32)
        two = xg[rows_at((2 * pair + 1) * (N_DP * ROWS) + s * 2 * ROWS, 2 * ROWS, 16)].astype(F32)
        at = s * 2 * TOK + pair * 2 * ROWS
        xc[rows_at(at, 2 * ROWS, 16)] = jnp.concatenate([one[:ROWS], two[:ROWS]], axis=0).astype(BF16)
        xc[rows_at(at + TOK, 2 * ROWS, 16)] = jnp.concatenate([one[ROWS:], two[ROWS:]], axis=0).astype(BF16)
        return carry

    def weight_copy(n):
        rows = pl.ds(n * 256, 256)
        return pltpu.make_async_copy(qw_ref.at[rows], qw_hbm.at[rows], l_s.at[4 + n])

    deep = 8 * TOK

    def weight_part(n, part):
        cols = slice(n * 256, (n + 1) * 256)
        rows = slice(part * deep, (part + 1) * deep)
        total = dot_tn(xc[rows, cols], grads[rows, :COLS])
        if part == 0:
            qw_ref[cols] = total
        else:
            qw_ref[cols] += total
            weight_copy(n).start()

    def pair_weights(n, carry):
        cols = rows_at(n * 256, 256, 256)
        total = dot_tn(grads[:, COLS:], xc[:, cols])
        kw_ref[:, cols] = total[:HALF]
        vw_ref[:, cols] = total[HALF:]
        return carry

    receive(1)
    begin(0)
    receive(8, 2, 6)
    second(0)
    receive(3)
    begin(1)
    receive(7)
    begin(2)
    receive(9)
    begin(3)
    receive(10, 14)
    third(0)
    second(1)
    receive(11)
    begin(4)
    second(2)
    receive(15)
    begin(5)
    third(1)
    last(0)
    second(3)
    tokens.wait(2)
    lax.fori_loop(0, 32, reorder, 0)
    third(2)
    last(1)
    second(4)
    receive(4, 12)
    third(3)
    last(2)
    second(5)
    receive(5)
    begin(6)
    receive(13)
    begin(7)
    third(4)
    last(3)
    weight_part(0, 0)
    third(5)
    last(4)
    second(6)
    weight_part(0, 1)
    second(7)
    last(5)
    weight_part(1, 0)
    third(6)
    weight_part(1, 1)
    third(7)
    last(6)
    weight_part(2, 0)
    weight_part(2, 1)
    last(7)
    weight_part(3, 0)
    weight_part(3, 1)
    lax.fori_loop(0, 4, pair_weights, 0)
    for s, base in enumerate(SLOTS):
        for e in range(2):
            n, mask = 2 * s + e, base ^ e
            if n:
                final_copy(n, mask).wait()
            gr_ref[:, rows_at(xor_dp(d, mask) * FEAT, FEAT, FEAT)] = unfold(done_in[n].astype(F32)).astype(BF16)
            if n:
                grad_arrival(mask).wait_send()
        for o in range(3):
            for stage in range(3):
                hop(s, o, stage).wait_send()
    weights.finish()
    tokens.finish()
    gq_out.wait()
    for n in range(4):
        weight_copy(n).wait()


def emit(*refs):
    count = len(refs) // 3
    sources, targets, held, (sem_in, sem_out) = refs[:count], refs[count : 2 * count], refs[2 * count : -2], refs[-2:]
    loads, stores = [], []
    for src, dst, mid in zip(sources, targets, held):
        parts = 4 if src.shape[0] >= FEAT else 1
        size = src.shape[0] // parts
        for n in range(parts):
            rows = pl.ds(n * size, size)
            loads.append(pltpu.make_async_copy(src.at[rows], mid.at[rows], sem_in.at[len(loads)]))
            stores.append(pltpu.make_async_copy(mid.at[rows], dst.at[rows], sem_out.at[len(stores)]))
    for load in loads:
        load.start()
    for load, store in zip(loads, stores):
        load.wait()
        store.start()
    for store in stores:
        store.wait()


def vmem(*shape, dtype=BF16):
    return pltpu.VMEM(shape, dtype)


def dma(*shape):
    return pltpu.SemaphoreType.DMA(shape)


def shards(x_rows, w_key, w_value, w_query, queries, grad_out, segment_ids):
    freqs = theta_base ** (-(2.0 * np.arange(HALF, dtype=np.float32)) / HD)
    freqs = jnp.asarray(freqs.astype(np.float32).reshape(1, HALF))
    in_vmem = pl.BlockSpec(memory_space=pltpu.VMEM)
    anywhere = pl.BlockSpec(memory_space=pl.ANY)
    shape = jax.ShapeDtypeStruct
    results = (
        shape((TOK, COLS), BF16), shape((ROWS, N_DP * FEAT), BF16), shape((HALF, FEAT), F32),
        shape((HALF, FEAT), F32), shape((FEAT, COLS), F32),
    )
    outs = pl.pallas_call(
        kernel,
        out_shape=results,
        in_specs=[in_vmem] * 5 + [anywhere] * 3,
        out_specs=(anywhere, in_vmem, in_vmem, in_vmem, anywhere),
        scratch_shapes=[
            vmem(TOK, COLS), vmem(TOK, COLS), vmem(FEAT, COLS), vmem(FEAT, COLS, dtype=F32),
            vmem(N_DP * TOK, FEAT), vmem(N_DP, ROWS, FEAT), vmem(1024, FEAT),
            vmem(N_DP * ROWS, 1024, dtype=F32), vmem(2, 8, 48, 512), vmem(8, 48, 512), vmem(8, 48, 512),
            vmem(4, 48, HD), vmem(N_T, 48, HD), vmem(2 * TOK, HD), vmem(2 * TOK, HD),
            vmem(TOK, HALF, dtype=F32), vmem(TOK, HALF, dtype=F32), vmem(TOK, TOK, dtype=F32),
            vmem(TOK, HD, dtype=F32), vmem(TOK, HD, dtype=F32), vmem(TOK, HD), vmem(TOK, HD),
            vmem(N_DP * TOK, WIDE), vmem(N_DP * TOK, FEAT), vmem(2 * TOK, FEAT, dtype=F32),
            vmem(8, 3, 128, 512), vmem(8, 3, 128, 512), vmem(8, 3, 128, 512),
            vmem(8, 3, 64, 512), vmem(8, 3, 64, 512), vmem(8, 3, 64, 512),
            vmem(8, 3, 32, 512), vmem(8, 3, 32, 512, dtype=F32), vmem(8, 3, 32, 512),
            vmem(N_DP, 48, 512), vmem(N_DP, 48, 512),
            dma(8), dma(N_DP), dma(N_DP), dma(3, 7), dma(3, 7), dma(3, 7), dma(3, 7),
            dma(8), dma(8), dma(N_T), dma(N_T), pltpu.SemaphoreType.DMA, pltpu.SemaphoreType.DMA,
            dma(N_DP), dma(N_DP), dma(N_DP), dma(N_DP),
            dma(8, 3), dma(8, 3), dma(8, 3), dma(8, 3), dma(8, 3), dma(8, 3),
        ],
        compiler_params=pltpu.CompilerParams(
            collective_id=0, has_side_effects=True, vmem_limit_bytes=62 * 2**20
        ),
        name="grads",
    )(x_rows, w_key.T, w_value.T, segment_ids, freqs, queries, grad_out, w_query)
    gq, rows, key_w, value_w, query_w = pl.pallas_call(
        emit,
        out_shape=results,
        in_specs=[anywhere] * 5,
        out_specs=(anywhere,) * 5,
        scratch_shapes=[pltpu.VMEM(r.shape, r.dtype) for r in results] + [dma(8), dma(8)],
        compiler_params=pltpu.CompilerParams(vmem_limit_bytes=62 * 2**20),
        name="emit",
    )(*outs)
    return (gq, rows, key_w.T, value_w.T, query_w)


def solution(mesh):
    placed = (
        P(("dp", "tensor"), None),
        P("dp", "tensor"),
        P("dp", "tensor"),
        P("dp", "tensor"),
        P("dp", "tensor"),
        P("dp", "tensor"),
        P("dp", None),
    )
    return jax.shard_map(
        shards,
        mesh=mesh,
        in_specs=placed,
        out_specs=(
            P("dp", "tensor"),
            P(("dp", "tensor"), None),
            P("dp", "tensor"),
            P("dp", "tensor"),
            P("dp", "tensor"),
        ),
        check_vma=False,
    )
```

```python
import jax
import jax.numpy as jnp
import numpy as np
from jax import lax
from jax.experimental import pallas as pl
from jax.experimental.pallas import tpu as pltpu
from jax.sharding import PartitionSpec as P

theta_base = 500000.0
MESH = pl.DeviceIdType.MESH
F32 = jnp.float32
BF16 = jnp.bfloat16

N_DP = 16
N_T = 8
ROWS = 24
TOK = 192
FEAT = 1024
COLS = 1024
HD = 128
HALF = 64
SLOTS = (0, 2, 6, 8, 10, 14, 4, 12)
ORDERS = ((1, 2, 6), (2, 6, 1), (6, 1, 2))
PARTS = ((0, 80), (80, 80), (160, 80), (240, 80), (320, 32), (352, 32))
PART_ORDERS = ((2, 1, 6), (6, 1, 2), (1, 2, 6), (1, 6, 2), (2, 6, 1), (6, 2, 1))


def xor_ring(place, mask):
    if mask == 0:
        return place
    if mask == 1:
        return place + 1 - 2 * lax.rem(place, 2)
    if mask == 2:
        return lax.rem(place + 2, 4)
    return 3 - place


def xor_dp(d, mask):
    y_hi, z, core = d // 8, lax.rem(d // 2, 4), lax.rem(d, 2)
    y_hi = 1 - y_hi if mask & 8 else y_hi
    core = 1 - core if mask & 1 else core
    return y_hi * 8 + xor_ring(z, (mask // 2) % 4) * 2 + core


def xor_t(t, mask):
    x, y_lo = t // 2, lax.rem(t, 2)
    y_lo = 1 - y_lo if mask & 1 else y_lo
    return xor_ring(x, mask // 2) * 2 + y_lo


def rows_at(start, size, unit):
    return pl.ds(pl.multiple_of(start, unit), size)


def remote(src, dst, send, recv, d, t):
    return pltpu.make_async_remote_copy(
        src_ref=src, dst_ref=dst, send_sem=send, recv_sem=recv, device_id=(d, t), device_id_type=MESH
    )


def fold(block):
    return jnp.concatenate([block[:, : FEAT // 2], block[:, FEAT // 2 :]], axis=0)


def unfold(block):
    return jnp.concatenate([block[:ROWS], block[ROWS:]], axis=1)


def dot_nt(a, b):
    return lax.dot_general(a, b, (((1,), (1,)), ((), ())), preferred_element_type=F32)


def dot_nn(a, b):
    return lax.dot_general(a, b, (((1,), (0,)), ((), ())), preferred_element_type=F32)


def dot_tn(a, b):
    return lax.dot_general(a, b, (((0,), (0,)), ((), ())), preferred_element_type=F32)


class Gather:
    def __init__(self, buf, slot_rows, chunks, orders, send, recv, d, t):
        self.buf, self.slot_rows, self.chunks, self.orders = buf, slot_rows, chunks, orders
        self.send, self.recv, self.d, self.t = send, recv, d, t

    def copies(self, stage, arriving, only=None):
        out = []
        for c in range(len(self.chunks)) if only is None else only:
            offset, size = self.chunks[c]
            first, second, third = self.orders[c]
            held = ([0], [0, first], [0, first, second, first ^ second])[stage]
            link = self.orders[c][stage]
            for j in held:
                slot = xor_t(self.t, j ^ link if arriving else j)
                part = self.buf.at[rows_at(slot * self.slot_rows + offset, size, 16)]
                n = (j ^ link) - 1
                out.append(
                    remote(part, part, self.send.at[c, n], self.recv.at[c, n], self.d, xor_t(self.t, link))
                )
        return out

    def start(self, stage):
        for copy in self.copies(stage, False):
            copy.start()

    def wait(self, stage):
        for copy in self.copies(stage, True):
            copy.wait_recv()

    def step(self, stage, only):
        for c in only:
            for copy in self.copies(stage, True, (c,)):
                copy.wait_recv()
            for copy in self.copies(stage + 1, False, (c,)):
                copy.start()

    def finish(self):
        for stage in range(3):
            for copy in self.copies(stage, False):
                copy.wait_send()


def kernel(
    x_ref, wk_ref, wv_ref, seg_ref, freq_ref, q_hbm, do_hbm, wq_hbm,
    gq_hbm, gr_ref, kw_ref, vw_ref, qw_hbm,
    q_ref, do_ref, wq_ref, qw_ref,
    xg, xa, wg, kvf, kvsend, kvswap, kvrecv, heads_out, heads_in, part_out, part_in,
    cos_ref, sin_ref, mask_ref, keyp, valuep, key_ref, value_ref,
    grads, owns, xc, term, s1, k1, r1, s2, k2, r2, s3, k3, r3, done_out, done_in,
    l_s, x_s, x_r, w_s, w_r, g_s, g_r, kv_s, kv_r, h_s, h_r, p_s, p_r,
    d_s, d_r, o_s, o_r, f_s, f_r, e1_s, e1_r, e2_s, e2_r, e3_s, e3_r,
):
    d = lax.axis_index("dp")
    t = lax.axis_index("tensor")
    barrier = pltpu.get_barrier_semaphore()

    def greet_dp(k, carry):
        pl.semaphore_signal(barrier, inc=1, device_id=(lax.rem(d + k, N_DP), t), device_id_type=MESH)
        return carry

    def greet_t(k, carry):
        pl.semaphore_signal(barrier, inc=1, device_id=(d, lax.rem(t + k, N_T)), device_id_type=MESH)
        return carry

    lax.fori_loop(1, N_DP, greet_dp, 0)
    lax.fori_loop(1, N_T, greet_t, 0)
    loads = [
        pltpu.make_async_copy(src, dst, l_s.at[n])
        for n, (src, dst) in enumerate(((q_hbm, q_ref), (do_hbm, do_ref), (wq_hbm, wq_ref)))
    ]
    for load in loads:
        load.start()
    wg[rows_at(t * HD, HALF, HALF)] = wk_ref[...]
    wg[rows_at(t * HD + HALF, HALF, HALF)] = wv_ref[...]
    pl.semaphore_wait(barrier, N_DP + N_T - 2)

    weights = Gather(wg, HD, ((0, 48), (48, 48), (96, 32)), ORDERS, w_s, w_r, d, t)
    weights.start(0)

    def x_copy(k):
        to = lax.rem(d + k, N_DP)
        return remote(
            x_ref.at[:, rows_at(to * FEAT, FEAT, FEAT)], xa.at[d], x_s.at[k], x_r.at[k], to, t
        )

    def send_x(k, carry):
        x_copy(k).start()
        return carry

    lax.fori_loop(1, N_DP, send_x, 0)
    weights.step(0, (1, 2, 0))
    weights.step(1, (1, 2, 0))
    xa[d] = x_ref[:, rows_at(d * FEAT, FEAT, FEAT)]

    row_no = lax.broadcasted_iota(jnp.int32, (TOK, TOK), 0)
    col_no = lax.broadcasted_iota(jnp.int32, (TOK, TOK), 1)
    seg_row = jnp.broadcast_to(seg_ref[...], (TOK, TOK))
    seg_col = jnp.sum(jnp.where(row_no == col_no, seg_row, 0), axis=1, keepdims=True)
    earlier = jnp.sum((seg_row < seg_col).astype(F32), axis=1, keepdims=True)
    place = lax.broadcasted_iota(jnp.int32, (TOK, 1), 0).astype(F32)
    angle = (place - earlier) * freq_ref[...]
    cos_ref[...] = jnp.cos(angle)
    sin_ref[...] = jnp.sin(angle)
    mask_ref[...] = ((seg_row == seg_col) & (col_no <= row_no)).astype(F32)

    def wait_x(k, carry):
        x_copy(k).wait_send()
        slot = xa.at[lax.rem(d + N_DP - k, N_DP)]
        remote(slot, slot, x_s.at[k], x_r.at[k], d, t).wait_recv()
        return carry

    lax.fori_loop(1, N_DP, wait_x, 0)
    for s, mask in enumerate(SLOTS):
        pair = [xa[xor_dp(d, mask ^ e)].astype(F32) for e in range(2)]
        xg[rows_at(t * (N_DP * ROWS) + s * 2 * ROWS, 2 * ROWS, 16)] = jnp.concatenate(pair, axis=0).astype(BF16)
    tokens = Gather(
        xg, N_DP * ROWS, PARTS, PART_ORDERS, g_s, g_r, d, t
    )
    tokens.start(0)

    weights.wait(2)

    def project(n, carry):
        own = xg[rows_at(t * (N_DP * ROWS), N_DP * ROWS, 16)]
        kvf[:, rows_at(n * 256, 256, 256)] = dot_nt(own, wg[rows_at(n * 256, 256, 256)])
        return carry

    lax.fori_loop(0, 4, project, 0)

    swap = remote(kvsend.at[1], kvswap, kv_s.at[0], kv_r.at[0], xor_dp(d, 1), t)

    def kv_copy(s):
        return remote(
            kvsend.at[0, s], kvrecv.at[s], kv_s.at[s], kv_r.at[s], xor_dp(d, SLOTS[s]), t
        )

    def kv_part(n):
        return fold(kvf[n * ROWS : (n + 1) * ROWS])

    for s in range(len(SLOTS)):
        kvsend[1, s] = kv_part(2 * s + 1).astype(BF16)
    swap.start()
    tokens.step(0, (4, 5, 0, 1))
    swap.wait()
    for s in range(1, len(SLOTS)):
        kvsend[0, s] = (kv_part(2 * s) + kvswap[s].astype(F32)).astype(BF16)
        kv_copy(s).start()
    tokens.step(0, (2, 3))
    lin = kv_part(0) + kvswap[0].astype(F32)
    for s in range(1, len(SLOTS)):
        kv_copy(s).wait()
        lin = lin + kvrecv[s].astype(F32)
    for head in range(4):
        rows = lin[(head // 2) * ROWS : (head // 2 + 1) * ROWS, (head % 2) * 256 : (head % 2 + 1) * 256]
        heads_out[head] = jnp.concatenate([rows[:, :HD], rows[:, HD:]], axis=0).astype(BF16)

    def head_copy(k, to):
        return remote(heads_out.at[to // 2], heads_in.at[t], h_s.at[k], h_r.at[k], d, to)

    def send_heads(k, carry):
        head_copy(k, lax.rem(t + k, N_T)).start()
        return carry

    lax.fori_loop(1, N_T, send_heads, 0)
    heads_in[t] = heads_out[t // 2]
    tokens.step(1, (0, 1, 2, 3))

    def wait_heads(k, carry):
        head_copy(k, lax.rem(t + k, N_T)).wait_send()
        slot = lax.rem(t + N_T - k, N_T)
        remote(heads_out.at[0], heads_in.at[slot], h_s.at[k], h_r.at[k], d, slot).wait_recv()
        return carry

    lax.fori_loop(1, N_T, wait_heads, 0)
    blocks = [heads_in[i].astype(F32) for i in range(N_T)]
    first = jnp.concatenate([b[:ROWS] for b in blocks], axis=0)
    second_part = jnp.concatenate([b[ROWS:] for b in blocks], axis=0)
    cosine, sine = cos_ref[...], sin_ref[...]
    a, c = first[:, :HALF], second_part[:, :HALF]
    key_ref[...] = jnp.concatenate([a * cosine - c * sine, c * cosine + a * sine], axis=1).astype(BF16)
    value_ref[...] = jnp.concatenate([first[:, HALF:], second_part[:, HALF:]], axis=1).astype(BF16)
    keyp[...] = jnp.zeros_like(keyp)
    valuep[...] = jnp.zeros_like(valuep)
    scale = 1.0 / HD**0.5
    for load in loads:
        load.wait()

    def head_step(i, carry):
        key, value = key_ref[...], value_ref[...]
        allowed = mask_ref[...] > 0.0
        for_key, for_value = [], []
        for e in range(2):
            cols = rows_at((2 * i + e) * HD, HD, HD)
            q, do = q_ref[:, cols], do_ref[:, cols]
            weight = jnp.where(allowed, jnp.exp(dot_nt(q, key) * scale), 0.0)
            probs = weight / jnp.sum(weight, axis=1, keepdims=True)
            dprob = dot_nt(do, value)
            delta = jnp.sum(probs * dprob, axis=1, keepdims=True)
            dscore = (probs * (dprob - delta)).astype(BF16)
            grads[0:TOK, cols] = (dot_nn(dscore, key) * scale).astype(BF16)
            for_key.append(dot_tn(dscore, q))
            for_value.append(dot_tn(probs.astype(BF16), do))
        keyp[...] += for_key[0] + for_key[1]
        valuep[...] += for_value[0] + for_value[1]
        return carry

    lax.fori_loop(0, 4, head_step, 0)
    place = {}
    for s, mask in enumerate(SLOTS):
        place[mask], place[mask ^ 1] = 2 * s, 2 * s + 1

    def block_of(buf, mask):
        return buf.at[pl.ds(place[mask] * TOK, TOK)]

    def grad_copy(buf, mask, link):
        there = mask ^ link
        n = place[there]
        send, recv = (d_s, d_r) if buf is grads else (o_s, o_r)
        return remote(block_of(buf, mask), block_of(buf, there), send.at[n], recv.at[n], xor_dp(d, link), t)

    def grad_arrival(buf, mask):
        n = place[mask]
        send, recv = (d_s, d_r) if buf is grads else (o_s, o_r)
        return remote(block_of(buf, mask), block_of(buf, mask), send.at[n], recv.at[n], xor_dp(d, 1), t)

    onward = {8: (2, 6, 1), 2: (1,), 6: (1,), 10: (1,), 14: (2, 1), 4: (1,), 12: (1,)}

    key_part = keyp[...] * scale
    part_out[0:TOK] = key_part.astype(BF16)
    part_out[TOK : 2 * TOK] = valuep[...].astype(BF16)
    part = remote(part_out, part_in, p_s, p_r, d, xor_t(t, 1))
    part.start()
    for link in (8, 2, 6, 1):
        grad_copy(grads, 0, link).start()
    gq_out = pltpu.make_async_copy(grads.at[0:TOK], gq_hbm, l_s.at[3])
    gq_out.start()
    part.wait()
    key_rot = key_part + part_in[0:TOK].astype(F32)
    value_sum = valuep[...] + part_in[TOK : 2 * TOK].astype(F32)
    upper, lower = key_rot[:, :HALF], key_rot[:, HALF:]
    is_first = lax.rem(t, 2) == 0
    own_key = jnp.where(is_first, upper * cosine + lower * sine, lower * cosine - upper * sine)
    own_value = jnp.where(is_first, value_sum[:, :HALF], value_sum[:, HALF:])
    owns[0:TOK] = jnp.concatenate([own_key, own_value], axis=1).astype(BF16)
    for link in (8, 2, 6, 1):
        grad_copy(owns, 0, link).start()

    def receive(*masks):
        for mask in masks:
            for buf in (grads, owns):
                grad_arrival(buf, mask).wait_recv()
                for link in onward.get(mask, ()):
                    grad_copy(buf, mask, link).start()
                if mask == 14:
                    grad_copy(buf, 2, 6).start()

    def multiply(s):
        def part(n, carry):
            cols = rows_at(n * 256, 256, 256)
            rows = slice(s * 2 * TOK, (s + 1) * 2 * TOK)
            total = dot_nt(grads[rows], wq_ref[rows_at(n * 256, 256, 256)])
            term[:, cols] = total + dot_nn(owns[rows], wg[rows_at(t * HD, HD, HD), cols])
            return carry

        lax.fori_loop(0, 4, part, 0)

    def split(s):
        for e in range(2):
            for j in range(N_T):
                start = e * TOK + ROWS * xor_t(t, j)
                piece = fold(term[rows_at(start, ROWS, 8)]).astype(BF16)
                for o, (g1, g2, g3) in enumerate(ORDERS):
                    kept = [0, g3, g2, g2 ^ g3]
                    to, q = (k1, kept.index(j)) if j in kept else (s1, kept.index(j ^ g1))
                    row = q * 32 + e * 16
                    to[s, o, row : row + 16] = piece[o * 16 : o * 16 + 16]

    def hop(s, o, stage):
        src, dst, send, recv = (
            (s1, r1, e1_s, e1_r), (s2, r2, e2_s, e2_r), (s3, r3, e3_s, e3_r)
        )[stage]
        return remote(
            src.at[s, o], dst.at[s, o], send.at[s, o], recv.at[s, o], d, xor_t(t, ORDERS[o][stage])
        )

    def begin(s):
        multiply(s)
        split(s)
        for o in range(3):
            hop(s, o, 0).start()

    def second(s):
        for o in range(3):
            hop(s, o, 0).wait_recv()
            s2[s, o] = (k1[s, o, 64:].astype(F32) + r1[s, o, 64:].astype(F32)).astype(BF16)
            hop(s, o, 1).start()
            k2[s, o] = (k1[s, o, :64].astype(F32) + r1[s, o, :64].astype(F32)).astype(BF16)

    def third(s):
        for o in range(3):
            hop(s, o, 1).wait_recv()
            s3[s, o] = (k2[s, o, 32:].astype(F32) + r2[s, o, 32:].astype(F32)).astype(BF16)
            hop(s, o, 2).start()
            k3[s, o] = k2[s, o, :32].astype(F32) + r2[s, o, :32].astype(F32)

    def final_copy(n, mask):
        return remote(done_out.at[n], done_in.at[n], f_s.at[n], f_r.at[n], xor_dp(d, mask), t)

    def last(s):
        for o in range(3):
            hop(s, o, 2).wait_recv()
            total = (k3[s, o] + r3[s, o].astype(F32)).astype(BF16)
            for e in range(2):
                to = done_in if 2 * s + e == 0 else done_out
                to[2 * s + e, o * 16 : o * 16 + 16] = total[e * 16 : e * 16 + 16]
        for e in range(2):
            if 2 * s + e:
                final_copy(2 * s + e, SLOTS[s] ^ e).start()

    def reorder(i, carry):
        s, pair = i // 4, lax.rem(i, 4)
        one = xg[rows_at((2 * pair) * (N_DP * ROWS) + s * 2 * ROWS, 2 * ROWS, 16)].astype(F32)
        two = xg[rows_at((2 * pair + 1) * (N_DP * ROWS) + s * 2 * ROWS, 2 * ROWS, 16)].astype(F32)
        at = s * 2 * TOK + pair * 2 * ROWS
        xc[rows_at(at, 2 * ROWS, 16)] = jnp.concatenate([one[:ROWS], two[:ROWS]], axis=0).astype(BF16)
        xc[rows_at(at + TOK, 2 * ROWS, 16)] = jnp.concatenate([one[ROWS:], two[ROWS:]], axis=0).astype(BF16)
        return carry

    def weight_copy(n):
        rows = pl.ds(n * 256, 256)
        return pltpu.make_async_copy(qw_ref.at[rows], qw_hbm.at[rows], l_s.at[4 + n])

    deep = 8 * TOK

    def weight_part(n, part):
        cols = slice(n * 256, (n + 1) * 256)
        rows = slice(part * deep, (part + 1) * deep)
        total = dot_tn(xc[rows, cols], grads[rows])
        if part == 0:
            qw_ref[cols] = total
        else:
            qw_ref[cols] += total
            weight_copy(n).start()

    def own_rows(*steps):
        for s in steps:
            for e in range(2):
                n, mask = 2 * s + e, SLOTS[s] ^ e
                if n:
                    final_copy(n, mask).wait_recv()
                cols = rows_at(xor_dp(d, mask) * FEAT, FEAT, FEAT)
                gr_ref[:, cols] = unfold(done_in[n].astype(F32)).astype(BF16)

    def pair_weights(n, carry):
        cols = rows_at(n * 256, 256, 256)
        total = dot_tn(owns[...], xc[:, cols])
        kw_ref[:, cols] = total[:HALF]
        vw_ref[:, cols] = total[HALF:]
        return carry

    receive(1)
    begin(0)
    receive(8)
    tokens.step(1, (4, 5))
    receive(2, 6)
    second(0)
    receive(3)
    begin(1)
    receive(7)
    begin(2)
    receive(9)
    begin(3)
    receive(10, 14)
    third(0)
    second(1)
    receive(11)
    begin(4)
    second(2)
    receive(15)
    begin(5)
    third(1)
    last(0)
    second(3)
    tokens.wait(2)
    lax.fori_loop(0, 32, reorder, 0)
    third(2)
    last(1)
    second(4)
    receive(4, 12)
    third(3)
    last(2)
    second(5)
    receive(5)
    begin(6)
    receive(13)
    begin(7)
    third(4)
    last(3)
    weight_part(0, 0)
    third(5)
    last(4)
    second(6)
    weight_part(0, 1)
    second(7)
    last(5)
    weight_part(1, 0)
    third(6)
    weight_part(1, 1)
    weight_part(2, 0)
    third(7)
    last(6)
    weight_part(2, 1)
    lax.fori_loop(0, 4, pair_weights, 0)
    own_rows(0, 1, 2, 3, 4)
    last(7)
    weight_part(3, 0)
    own_rows(5)
    weight_part(3, 1)
    own_rows(6, 7)
    for s, base in enumerate(SLOTS):
        for e in range(2):
            if 2 * s + e:
                final_copy(2 * s + e, base ^ e).wait_send()
                grad_arrival(grads, base ^ e).wait_send()
                grad_arrival(owns, base ^ e).wait_send()
        for o in range(3):
            for stage in range(3):
                hop(s, o, stage).wait_send()
    weights.finish()
    tokens.finish()
    gq_out.wait()
    for n in range(4):
        weight_copy(n).wait()


def emit(*refs):
    count = len(refs) // 3
    sources, targets, held, (sem_in, sem_out) = refs[:count], refs[count : 2 * count], refs[2 * count : -2], refs[-2:]
    loads, stores = [], []
    for src, dst, mid in zip(sources, targets, held):
        parts = 4 if src.shape[0] >= FEAT else 1
        size = src.shape[0] // parts
        for n in range(parts):
            rows = pl.ds(n * size, size)
            loads.append(pltpu.make_async_copy(src.at[rows], mid.at[rows], sem_in.at[len(loads)]))
            stores.append(pltpu.make_async_copy(mid.at[rows], dst.at[rows], sem_out.at[len(stores)]))
    for load in loads:
        load.start()
    for load, store in zip(loads, stores):
        load.wait()
        store.start()
    for store in stores:
        store.wait()


def vmem(*shape, dtype=BF16):
    return pltpu.VMEM(shape, dtype)


def dma(*shape):
    return pltpu.SemaphoreType.DMA(shape)


def shards(x_rows, w_key, w_value, w_query, queries, grad_out, segment_ids):
    freqs = theta_base ** (-(2.0 * np.arange(HALF, dtype=np.float32)) / HD)
    freqs = jnp.asarray(freqs.astype(np.float32).reshape(1, HALF))
    in_vmem = pl.BlockSpec(memory_space=pltpu.VMEM)
    anywhere = pl.BlockSpec(memory_space=pl.ANY)
    shape = jax.ShapeDtypeStruct
    results = (
        shape((TOK, COLS), BF16), shape((ROWS, N_DP * FEAT), BF16), shape((HALF, FEAT), F32),
        shape((HALF, FEAT), F32), shape((FEAT, COLS), F32),
    )
    outs = pl.pallas_call(
        kernel,
        out_shape=results,
        in_specs=[in_vmem] * 5 + [anywhere] * 3,
        out_specs=(anywhere, in_vmem, in_vmem, in_vmem, anywhere),
        scratch_shapes=[
            vmem(TOK, COLS), vmem(TOK, COLS), vmem(FEAT, COLS), vmem(FEAT, COLS, dtype=F32),
            vmem(N_DP * TOK, FEAT), vmem(N_DP, ROWS, FEAT), vmem(1024, FEAT),
            vmem(N_DP * ROWS, 1024, dtype=F32), vmem(2, 8, 48, 512), vmem(8, 48, 512), vmem(8, 48, 512),
            vmem(4, 48, HD), vmem(N_T, 48, HD), vmem(2 * TOK, HD), vmem(2 * TOK, HD),
            vmem(TOK, HALF, dtype=F32), vmem(TOK, HALF, dtype=F32), vmem(TOK, TOK, dtype=F32),
            vmem(TOK, HD, dtype=F32), vmem(TOK, HD, dtype=F32), vmem(TOK, HD), vmem(TOK, HD),
            vmem(N_DP * TOK, COLS), vmem(N_DP * TOK, HD), vmem(N_DP * TOK, FEAT), vmem(2 * TOK, FEAT, dtype=F32),
            vmem(8, 3, 128, 512), vmem(8, 3, 128, 512), vmem(8, 3, 128, 512),
            vmem(8, 3, 64, 512), vmem(8, 3, 64, 512), vmem(8, 3, 64, 512),
            vmem(8, 3, 32, 512), vmem(8, 3, 32, 512, dtype=F32), vmem(8, 3, 32, 512),
            vmem(N_DP, 48, 512), vmem(N_DP, 48, 512),
            dma(8), dma(N_DP), dma(N_DP), dma(3, 7), dma(3, 7), dma(6, 7), dma(6, 7),
            dma(8), dma(8), dma(N_T), dma(N_T), pltpu.SemaphoreType.DMA, pltpu.SemaphoreType.DMA,
            dma(N_DP), dma(N_DP), dma(N_DP), dma(N_DP), dma(N_DP), dma(N_DP),
            dma(8, 3), dma(8, 3), dma(8, 3), dma(8, 3), dma(8, 3), dma(8, 3),
        ],
        compiler_params=pltpu.CompilerParams(
            collective_id=0, has_side_effects=True, vmem_limit_bytes=62 * 2**20
        ),
        name="grads",
    )(x_rows, w_key.T, w_value.T, segment_ids, freqs, queries, grad_out, w_query)
    gq, rows, key_w, value_w, query_w = pl.pallas_call(
        emit,
        out_shape=results,
        in_specs=[anywhere] * 5,
        out_specs=(anywhere,) * 5,
        scratch_shapes=[pltpu.VMEM(r.shape, r.dtype) for r in results] + [dma(8), dma(8)],
        compiler_params=pltpu.CompilerParams(vmem_limit_bytes=62 * 2**20),
        name="emit",
    )(*outs)
    return (gq, rows, key_w.T, value_w.T, query_w)


def solution(mesh):
    placed = (
        P(("dp", "tensor"), None),
        P("dp", "tensor"),
        P("dp", "tensor"),
        P("dp", "tensor"),
        P("dp", "tensor"),
        P("dp", "tensor"),
        P("dp", None),
    )
    return jax.shard_map(
        shards,
        mesh=mesh,
        in_specs=placed,
        out_specs=(
            P("dp", "tensor"),
            P(("dp", "tensor"), None),
            P("dp", "tensor"),
            P("dp", "tensor"),
            P("dp", "tensor"),
        ),
        check_vma=False,
    )
```

```python
import jax
import jax.numpy as jnp
import numpy as np
from jax import lax
from jax.experimental import pallas as pl
from jax.experimental.pallas import tpu as pltpu
from jax.sharding import PartitionSpec as P

theta_base = 500000.0
MESH = pl.DeviceIdType.MESH
F32 = jnp.float32
BF16 = jnp.bfloat16

N_DP = 16
N_T = 8
ROWS = 24
TOK = 192
FEAT = 1024
COLS = 1024
HD = 128
HALF = 64
SLOTS = (0, 2, 6, 8, 10, 14, 4, 12)
ORDERS = ((1, 2, 6), (2, 6, 1), (6, 1, 2))
PARTS = ((0, 80), (80, 80), (160, 80), (240, 80), (320, 32), (352, 32))
PART_ORDERS = ((2, 1, 6), (6, 1, 2), (1, 2, 6), (1, 6, 2), (2, 6, 1), (6, 2, 1))


def xor_ring(place, mask):
    if mask == 0:
        return place
    if mask == 1:
        return place + 1 - 2 * lax.rem(place, 2)
    if mask == 2:
        return lax.rem(place + 2, 4)
    return 3 - place


def xor_dp(d, mask):
    y_hi, z, core = d // 8, lax.rem(d // 2, 4), lax.rem(d, 2)
    y_hi = 1 - y_hi if mask & 8 else y_hi
    core = 1 - core if mask & 1 else core
    return y_hi * 8 + xor_ring(z, (mask // 2) % 4) * 2 + core


def xor_t(t, mask):
    x, y_lo = t // 2, lax.rem(t, 2)
    y_lo = 1 - y_lo if mask & 1 else y_lo
    return xor_ring(x, mask // 2) * 2 + y_lo


def rows_at(start, size, unit):
    return pl.ds(pl.multiple_of(start, unit), size)


def remote(src, dst, send, recv, d, t):
    return pltpu.make_async_remote_copy(
        src_ref=src, dst_ref=dst, send_sem=send, recv_sem=recv, device_id=(d, t), device_id_type=MESH
    )


def fold(block):
    return jnp.concatenate([block[:, : FEAT // 2], block[:, FEAT // 2 :]], axis=0)


def unfold(block):
    return jnp.concatenate([block[:ROWS], block[ROWS:]], axis=1)


def dot_nt(a, b):
    return lax.dot_general(a, b, (((1,), (1,)), ((), ())), preferred_element_type=F32)


def dot_nn(a, b):
    return lax.dot_general(a, b, (((1,), (0,)), ((), ())), preferred_element_type=F32)


def dot_tn(a, b):
    return lax.dot_general(a, b, (((0,), (0,)), ((), ())), preferred_element_type=F32)


class Gather:
    def __init__(self, buf, slot_rows, chunks, orders, send, recv, d, t):
        self.buf, self.slot_rows, self.chunks, self.orders = buf, slot_rows, chunks, orders
        self.send, self.recv, self.d, self.t = send, recv, d, t

    def copies(self, stage, arriving, only=None):
        out = []
        for c in range(len(self.chunks)) if only is None else only:
            offset, size = self.chunks[c]
            first, second, third = self.orders[c]
            held = ([0], [0, first], [0, first, second, first ^ second])[stage]
            link = self.orders[c][stage]
            for j in held:
                slot = xor_t(self.t, j ^ link if arriving else j)
                part = self.buf.at[rows_at(slot * self.slot_rows + offset, size, 16)]
                n = (j ^ link) - 1
                out.append(
                    remote(part, part, self.send.at[c, n], self.recv.at[c, n], self.d, xor_t(self.t, link))
                )
        return out

    def start(self, stage):
        for copy in self.copies(stage, False):
            copy.start()

    def wait(self, stage):
        for copy in self.copies(stage, True):
            copy.wait_recv()

    def step(self, stage, only):
        for c in only:
            for copy in self.copies(stage, True, (c,)):
                copy.wait_recv()
            for copy in self.copies(stage + 1, False, (c,)):
                copy.start()

    def finish(self):
        for stage in range(3):
            for copy in self.copies(stage, False):
                copy.wait_send()


def kernel(
    x_ref, wk_ref, wv_ref, seg_ref, freq_ref, q_hbm, do_hbm, wq_hbm,
    gq_hbm, gr_ref, kw_ref, vw_ref, qw_hbm,
    q_ref, do_ref, wq_ref, qw_ref,
    xg, xa, wg, kvf, kvsend, kvswap, kvrecv, heads_out, heads_in, part_out, part_in,
    cos_ref, sin_ref, mask_ref, keyp, valuep, key_ref, value_ref,
    grads, owns, xc, term, s1, k1, r1, s2, k2, r2, s3, k3, r3, done_out, done_in,
    l_s, x_s, x_r, w_s, w_r, g_s, g_r, kv_s, kv_r, h_s, h_r, p_s, p_r,
    d_s, d_r, o_s, o_r, f_s, f_r, e1_s, e1_r, e2_s, e2_r, e3_s, e3_r,
):
    d = lax.axis_index("dp")
    t = lax.axis_index("tensor")
    barrier = pltpu.get_barrier_semaphore()

    def greet_dp(k, carry):
        pl.semaphore_signal(barrier, inc=1, device_id=(lax.rem(d + k, N_DP), t), device_id_type=MESH)
        return carry

    def greet_t(k, carry):
        pl.semaphore_signal(barrier, inc=1, device_id=(d, lax.rem(t + k, N_T)), device_id_type=MESH)
        return carry

    lax.fori_loop(1, N_DP, greet_dp, 0)
    lax.fori_loop(1, N_T, greet_t, 0)
    loads = [
        pltpu.make_async_copy(src, dst, l_s.at[n])
        for n, (src, dst) in enumerate(((q_hbm, q_ref), (do_hbm, do_ref), (wq_hbm, wq_ref)))
    ]
    for load in loads:
        load.start()
    wg[rows_at(t * HD, HALF, HALF)] = wk_ref[...]
    wg[rows_at(t * HD + HALF, HALF, HALF)] = wv_ref[...]
    pl.semaphore_wait(barrier, N_DP + N_T - 2)

    weights = Gather(wg, HD, ((0, 48), (48, 48), (96, 32)), ORDERS, w_s, w_r, d, t)
    weights.start(0)

    def x_copy(k):
        to = lax.rem(d + k, N_DP)
        return remote(
            x_ref.at[:, rows_at(to * FEAT, FEAT, FEAT)], xa.at[d], x_s.at[k], x_r.at[k], to, t
        )

    def send_x(k, carry):
        x_copy(k).start()
        return carry

    lax.fori_loop(1, N_DP, send_x, 0)
    weights.step(0, (1, 2, 0))
    weights.step(1, (1, 2, 0))
    xa[d] = x_ref[:, rows_at(d * FEAT, FEAT, FEAT)]

    row_no = lax.broadcasted_iota(jnp.int32, (TOK, TOK), 0)
    col_no = lax.broadcasted_iota(jnp.int32, (TOK, TOK), 1)
    seg_row = jnp.broadcast_to(seg_ref[...], (TOK, TOK))
    seg_col = jnp.sum(jnp.where(row_no == col_no, seg_row, 0), axis=1, keepdims=True)
    earlier = jnp.sum((seg_row < seg_col).astype(F32), axis=1, keepdims=True)
    place = lax.broadcasted_iota(jnp.int32, (TOK, 1), 0).astype(F32)
    angle = (place - earlier) * freq_ref[...]
    cos_ref[...] = jnp.cos(angle)
    sin_ref[...] = jnp.sin(angle)
    mask_ref[...] = ((seg_row == seg_col) & (col_no <= row_no)).astype(F32)

    def wait_x(k, carry):
        x_copy(k).wait_send()
        slot = xa.at[lax.rem(d + N_DP - k, N_DP)]
        remote(slot, slot, x_s.at[k], x_r.at[k], d, t).wait_recv()
        return carry

    lax.fori_loop(1, N_DP, wait_x, 0)
    for s, mask in enumerate(SLOTS):
        pair = [xa[xor_dp(d, mask ^ e)].astype(F32) for e in range(2)]
        xg[rows_at(t * (N_DP * ROWS) + s * 2 * ROWS, 2 * ROWS, 16)] = jnp.concatenate(pair, axis=0).astype(BF16)
    tokens = Gather(
        xg, N_DP * ROWS, PARTS, PART_ORDERS, g_s, g_r, d, t
    )
    tokens.start(0)

    weights.wait(2)

    def project(n, carry):
        own = xg[rows_at(t * (N_DP * ROWS), N_DP * ROWS, 16)]
        kvf[:, rows_at(n * 256, 256, 256)] = dot_nt(own, wg[rows_at(n * 256, 256, 256)])
        return carry

    lax.fori_loop(0, 4, project, 0)

    swap = remote(kvsend.at[1], kvswap, kv_s.at[0], kv_r.at[0], xor_dp(d, 1), t)

    def kv_copy(s):
        return remote(
            kvsend.at[0, s], kvrecv.at[s], kv_s.at[s], kv_r.at[s], xor_dp(d, SLOTS[s]), t
        )

    def kv_part(n):
        return fold(kvf[n * ROWS : (n + 1) * ROWS])

    for s in range(len(SLOTS)):
        kvsend[1, s] = kv_part(2 * s + 1).astype(BF16)
    swap.start()
    tokens.step(0, (4, 5, 0, 1))
    swap.wait()
    for s in range(1, len(SLOTS)):
        kvsend[0, s] = (kv_part(2 * s) + kvswap[s].astype(F32)).astype(BF16)
        kv_copy(s).start()
    tokens.step(0, (2, 3))
    lin = kv_part(0) + kvswap[0].astype(F32)
    for s in range(1, len(SLOTS)):
        kv_copy(s).wait()
        lin = lin + kvrecv[s].astype(F32)
    for head in range(4):
        rows = lin[(head // 2) * ROWS : (head // 2 + 1) * ROWS, (head % 2) * 256 : (head % 2 + 1) * 256]
        heads_out[head] = jnp.concatenate([rows[:, :HD], rows[:, HD:]], axis=0).astype(BF16)

    def head_copy(k, to):
        return remote(heads_out.at[to // 2], heads_in.at[t], h_s.at[k], h_r.at[k], d, to)

    def send_heads(k, carry):
        head_copy(k, lax.rem(t + k, N_T)).start()
        return carry

    lax.fori_loop(1, N_T, send_heads, 0)
    heads_in[t] = heads_out[t // 2]
    tokens.step(1, (0, 1, 2, 3))

    def wait_heads(k, carry):
        head_copy(k, lax.rem(t + k, N_T)).wait_send()
        slot = lax.rem(t + N_T - k, N_T)
        remote(heads_out.at[0], heads_in.at[slot], h_s.at[k], h_r.at[k], d, slot).wait_recv()
        return carry

    lax.fori_loop(1, N_T, wait_heads, 0)
    blocks = [heads_in[i].astype(F32) for i in range(N_T)]
    first = jnp.concatenate([b[:ROWS] for b in blocks], axis=0)
    second_part = jnp.concatenate([b[ROWS:] for b in blocks], axis=0)
    cosine, sine = cos_ref[...], sin_ref[...]
    a, c = first[:, :HALF], second_part[:, :HALF]
    key_ref[...] = jnp.concatenate([a * cosine - c * sine, c * cosine + a * sine], axis=1).astype(BF16)
    value_ref[...] = jnp.concatenate([first[:, HALF:], second_part[:, HALF:]], axis=1).astype(BF16)
    keyp[...] = jnp.zeros_like(keyp)
    valuep[...] = jnp.zeros_like(valuep)
    scale = 1.0 / HD**0.5
    for load in loads:
        load.wait()

    def head_step(i, carry):
        key, value = key_ref[...], value_ref[...]
        allowed = mask_ref[...] > 0.0
        for_key, for_value = [], []
        for e in range(2):
            cols = rows_at((2 * i + e) * HD, HD, HD)
            q, do = q_ref[:, cols], do_ref[:, cols]
            weight = jnp.where(allowed, jnp.exp(dot_nt(q, key) * scale), 0.0)
            probs = weight / jnp.sum(weight, axis=1, keepdims=True)
            dprob = dot_nt(do, value)
            delta = jnp.sum(probs * dprob, axis=1, keepdims=True)
            dscore = (probs * (dprob - delta)).astype(BF16)
            grads[0:TOK, cols] = (dot_nn(dscore, key) * scale).astype(BF16)
            for_key.append(dot_tn(dscore, q))
            for_value.append(dot_tn(probs.astype(BF16), do))
        keyp[...] += for_key[0] + for_key[1]
        valuep[...] += for_value[0] + for_value[1]
        return carry

    lax.fori_loop(0, 4, head_step, 0)
    place = {}
    for s, mask in enumerate(SLOTS):
        place[mask], place[mask ^ 1] = 2 * s, 2 * s + 1

    def block_of(buf, mask):
        return buf.at[pl.ds(place[mask] * TOK, TOK)]

    def grad_copy(buf, mask, link):
        there = mask ^ link
        n = place[there]
        send, recv = (d_s, d_r) if buf is grads else (o_s, o_r)
        return remote(block_of(buf, mask), block_of(buf, there), send.at[n], recv.at[n], xor_dp(d, link), t)

    def grad_arrival(buf, mask):
        n = place[mask]
        send, recv = (d_s, d_r) if buf is grads else (o_s, o_r)
        return remote(block_of(buf, mask), block_of(buf, mask), send.at[n], recv.at[n], xor_dp(d, 1), t)

    onward = {8: (2, 6, 1), 2: (1,), 6: (1,), 10: (1,), 14: (2, 1), 4: (1,), 12: (1,)}

    key_part = keyp[...] * scale
    part_out[0:TOK] = key_part.astype(BF16)
    part_out[TOK : 2 * TOK] = valuep[...].astype(BF16)
    part = remote(part_out, part_in, p_s, p_r, d, xor_t(t, 1))
    part.start()
    for link in (8, 2, 6, 1):
        grad_copy(grads, 0, link).start()
    gq_out = pltpu.make_async_copy(grads.at[0:TOK], gq_hbm, l_s.at[3])
    gq_out.start()
    part.wait()
    key_rot = key_part + part_in[0:TOK].astype(F32)
    value_sum = valuep[...] + part_in[TOK : 2 * TOK].astype(F32)
    upper, lower = key_rot[:, :HALF], key_rot[:, HALF:]
    is_first = lax.rem(t, 2) == 0
    own_key = jnp.where(is_first, upper * cosine + lower * sine, lower * cosine - upper * sine)
    own_value = jnp.where(is_first, value_sum[:, :HALF], value_sum[:, HALF:])
    owns[0:TOK] = jnp.concatenate([own_key, own_value], axis=1).astype(BF16)
    for link in (8, 2, 6, 1):
        grad_copy(owns, 0, link).start()

    def receive(*masks):
        for mask in masks:
            for buf in (grads, owns):
                grad_arrival(buf, mask).wait_recv()
                for link in onward.get(mask, ()):
                    grad_copy(buf, mask, link).start()
                if mask == 14:
                    grad_copy(buf, 2, 6).start()

    def multiply(s):
        def part(n, carry):
            cols = rows_at(n * 256, 256, 256)
            rows = slice(s * 2 * TOK, (s + 1) * 2 * TOK)
            total = dot_nt(grads[rows], wq_ref[rows_at(n * 256, 256, 256)])
            term[:, cols] = total + dot_nn(owns[rows], wg[rows_at(t * HD, HD, HD), cols])
            return carry

        lax.fori_loop(0, 4, part, 0)

    def split(s):
        for e in range(2):
            for j in range(N_T):
                start = e * TOK + ROWS * xor_t(t, j)
                piece = fold(term[rows_at(start, ROWS, 8)]).astype(BF16)
                for o, (g1, g2, g3) in enumerate(ORDERS):
                    kept = [0, g3, g2, g2 ^ g3]
                    to, q = (k1, kept.index(j)) if j in kept else (s1, kept.index(j ^ g1))
                    row = q * 32 + e * 16
                    to[s, o, row : row + 16] = piece[o * 16 : o * 16 + 16]

    def hop(s, o, stage):
        src, dst, send, recv = (
            (s1, r1, e1_s, e1_r), (s2, r2, e2_s, e2_r), (s3, r3, e3_s, e3_r)
        )[stage]
        return remote(
            src.at[s, o], dst.at[s, o], send.at[s, o], recv.at[s, o], d, xor_t(t, ORDERS[o][stage])
        )

    def begin(s):
        multiply(s)
        split(s)
        for o in range(3):
            hop(s, o, 0).start()

    def second(s):
        for o in range(3):
            hop(s, o, 0).wait_recv()
            s2[s, o] = (k1[s, o, 64:].astype(F32) + r1[s, o, 64:].astype(F32)).astype(BF16)
            hop(s, o, 1).start()
            k2[s, o] = (k1[s, o, :64].astype(F32) + r1[s, o, :64].astype(F32)).astype(BF16)

    def third(s):
        for o in range(3):
            hop(s, o, 1).wait_recv()
            s3[s, o] = (k2[s, o, 32:].astype(F32) + r2[s, o, 32:].astype(F32)).astype(BF16)
            hop(s, o, 2).start()
            k3[s, o] = k2[s, o, :32].astype(F32) + r2[s, o, :32].astype(F32)

    def final_copy(n, mask):
        return remote(done_out.at[n], done_in.at[n], f_s.at[n], f_r.at[n], xor_dp(d, mask), t)

    def last(s):
        for o in range(3):
            hop(s, o, 2).wait_recv()
            total = (k3[s, o] + r3[s, o].astype(F32)).astype(BF16)
            for e in range(2):
                to = done_in if 2 * s + e == 0 else done_out
                to[2 * s + e, o * 16 : o * 16 + 16] = total[e * 16 : e * 16 + 16]
        for e in range(2):
            if 2 * s + e:
                final_copy(2 * s + e, SLOTS[s] ^ e).start()

    def reorder(i, carry):
        s, pair = i // 4, lax.rem(i, 4)
        one = xg[rows_at((2 * pair) * (N_DP * ROWS) + s * 2 * ROWS, 2 * ROWS, 16)].astype(F32)
        two = xg[rows_at((2 * pair + 1) * (N_DP * ROWS) + s * 2 * ROWS, 2 * ROWS, 16)].astype(F32)
        at = s * 2 * TOK + pair * 2 * ROWS
        xc[rows_at(at, 2 * ROWS, 16)] = jnp.concatenate([one[:ROWS], two[:ROWS]], axis=0).astype(BF16)
        xc[rows_at(at + TOK, 2 * ROWS, 16)] = jnp.concatenate([one[ROWS:], two[ROWS:]], axis=0).astype(BF16)
        return carry

    def weight_copy(n):
        rows = pl.ds(n * 256, 256)
        return pltpu.make_async_copy(qw_ref.at[rows], qw_hbm.at[rows], l_s.at[4 + n])

    deep = 8 * TOK

    def weight_part(n, part):
        cols = slice(n * 256, (n + 1) * 256)
        rows = slice(part * deep, (part + 1) * deep)
        total = dot_tn(xc[rows, cols], grads[rows])
        if part == 0:
            qw_ref[cols] = total
        else:
            qw_ref[cols] += total
            weight_copy(n).start()

    def pair_weights(n, carry):
        cols = rows_at(n * 256, 256, 256)
        total = dot_tn(owns[...], xc[:, cols])
        kw_ref[:, cols] = total[:HALF]
        vw_ref[:, cols] = total[HALF:]
        return carry

    receive(1)
    begin(0)
    receive(8)
    tokens.step(1, (4, 5))
    receive(2, 6)
    second(0)
    receive(3)
    begin(1)
    receive(7)
    begin(2)
    receive(9)
    begin(3)
    receive(10, 14)
    third(0)
    second(1)
    receive(11)
    begin(4)
    second(2)
    receive(15)
    begin(5)
    third(1)
    last(0)
    second(3)
    tokens.wait(2)
    lax.fori_loop(0, 32, reorder, 0)
    third(2)
    last(1)
    second(4)
    receive(4, 12)
    third(3)
    last(2)
    second(5)
    receive(5)
    begin(6)
    receive(13)
    begin(7)
    third(4)
    last(3)
    weight_part(0, 0)
    third(5)
    last(4)
    second(6)
    weight_part(0, 1)
    second(7)
    last(5)
    weight_part(1, 0)
    third(6)
    weight_part(1, 1)
    third(7)
    last(6)
    weight_part(2, 0)
    weight_part(2, 1)
    last(7)
    weight_part(3, 0)
    weight_part(3, 1)
    lax.fori_loop(0, 4, pair_weights, 0)
    for s, base in enumerate(SLOTS):
        for e in range(2):
            n, mask = 2 * s + e, base ^ e
            if n:
                final_copy(n, mask).wait()
            gr_ref[:, rows_at(xor_dp(d, mask) * FEAT, FEAT, FEAT)] = unfold(done_in[n].astype(F32)).astype(BF16)
            if n:
                grad_arrival(grads, mask).wait_send()
                grad_arrival(owns, mask).wait_send()
        for o in range(3):
            for stage in range(3):
                hop(s, o, stage).wait_send()
    weights.finish()
    tokens.finish()
    gq_out.wait()
    for n in range(4):
        weight_copy(n).wait()


def emit(*refs):
    count = len(refs) // 3
    sources, targets, held, (sem_in, sem_out) = refs[:count], refs[count : 2 * count], refs[2 * count : -2], refs[-2:]
    loads, stores = [], []
    for src, dst, mid in zip(sources, targets, held):
        parts = 4 if src.shape[0] >= FEAT else 1
        size = src.shape[0] // parts
        for n in range(parts):
            rows = pl.ds(n * size, size)
            loads.append(pltpu.make_async_copy(src.at[rows], mid.at[rows], sem_in.at[len(loads)]))
            stores.append(pltpu.make_async_copy(mid.at[rows], dst.at[rows], sem_out.at[len(stores)]))
    for load in loads:
        load.start()
    for load, store in zip(loads, stores):
        load.wait()
        store.start()
    for store in stores:
        store.wait()


def vmem(*shape, dtype=BF16):
    return pltpu.VMEM(shape, dtype)


def dma(*shape):
    return pltpu.SemaphoreType.DMA(shape)


def shards(x_rows, w_key, w_value, w_query, queries, grad_out, segment_ids):
    freqs = theta_base ** (-(2.0 * np.arange(HALF, dtype=np.float32)) / HD)
    freqs = jnp.asarray(freqs.astype(np.float32).reshape(1, HALF))
    in_vmem = pl.BlockSpec(memory_space=pltpu.VMEM)
    anywhere = pl.BlockSpec(memory_space=pl.ANY)
    shape = jax.ShapeDtypeStruct
    results = (
        shape((TOK, COLS), BF16), shape((ROWS, N_DP * FEAT), BF16), shape((HALF, FEAT), F32),
        shape((HALF, FEAT), F32), shape((FEAT, COLS), F32),
    )
    outs = pl.pallas_call(
        kernel,
        out_shape=results,
        in_specs=[in_vmem] * 5 + [anywhere] * 3,
        out_specs=(anywhere, in_vmem, in_vmem, in_vmem, anywhere),
        scratch_shapes=[
            vmem(TOK, COLS), vmem(TOK, COLS), vmem(FEAT, COLS), vmem(FEAT, COLS, dtype=F32),
            vmem(N_DP * TOK, FEAT), vmem(N_DP, ROWS, FEAT), vmem(1024, FEAT),
            vmem(N_DP * ROWS, 1024, dtype=F32), vmem(2, 8, 48, 512), vmem(8, 48, 512), vmem(8, 48, 512),
            vmem(4, 48, HD), vmem(N_T, 48, HD), vmem(2 * TOK, HD), vmem(2 * TOK, HD),
            vmem(TOK, HALF, dtype=F32), vmem(TOK, HALF, dtype=F32), vmem(TOK, TOK, dtype=F32),
            vmem(TOK, HD, dtype=F32), vmem(TOK, HD, dtype=F32), vmem(TOK, HD), vmem(TOK, HD),
            vmem(N_DP * TOK, COLS), vmem(N_DP * TOK, HD), vmem(N_DP * TOK, FEAT), vmem(2 * TOK, FEAT, dtype=F32),
            vmem(8, 3, 128, 512), vmem(8, 3, 128, 512), vmem(8, 3, 128, 512),
            vmem(8, 3, 64, 512), vmem(8, 3, 64, 512), vmem(8, 3, 64, 512),
            vmem(8, 3, 32, 512), vmem(8, 3, 32, 512, dtype=F32), vmem(8, 3, 32, 512),
            vmem(N_DP, 48, 512), vmem(N_DP, 48, 512),
            dma(8), dma(N_DP), dma(N_DP), dma(3, 7), dma(3, 7), dma(6, 7), dma(6, 7),
            dma(8), dma(8), dma(N_T), dma(N_T), pltpu.SemaphoreType.DMA, pltpu.SemaphoreType.DMA,
            dma(N_DP), dma(N_DP), dma(N_DP), dma(N_DP), dma(N_DP), dma(N_DP),
            dma(8, 3), dma(8, 3), dma(8, 3), dma(8, 3), dma(8, 3), dma(8, 3),
        ],
        compiler_params=pltpu.CompilerParams(
            collective_id=0, has_side_effects=True, vmem_limit_bytes=62 * 2**20
        ),
        name="grads",
    )(x_rows, w_key.T, w_value.T, segment_ids, freqs, queries, grad_out, w_query)
    gq, rows, key_w, value_w, query_w = pl.pallas_call(
        emit,
        out_shape=results,
        in_specs=[anywhere] * 5,
        out_specs=(anywhere,) * 5,
        scratch_shapes=[pltpu.VMEM(r.shape, r.dtype) for r in results] + [dma(8), dma(8)],
        compiler_params=pltpu.CompilerParams(vmem_limit_bytes=62 * 2**20),
        name="emit",
    )(*outs)
    return (gq, rows, key_w.T, value_w.T, query_w)


def solution(mesh):
    placed = (
        P(("dp", "tensor"), None),
        P("dp", "tensor"),
        P("dp", "tensor"),
        P("dp", "tensor"),
        P("dp", "tensor"),
        P("dp", "tensor"),
        P("dp", None),
    )
    return jax.shard_map(
        shards,
        mesh=mesh,
        in_specs=placed,
        out_specs=(
            P("dp", "tensor"),
            P(("dp", "tensor"), None),
            P("dp", "tensor"),
            P("dp", "tensor"),
            P("dp", "tensor"),
        ),
        check_vma=False,
    )
```
